512 devices in a mesh: tm: 8 (over x, y_lo), height: 64 (over z, y_hi, core).
Axes of the slice: x: 4, y: 4 (y_hi: 2, y_lo: 2; y = y_hi * 2 + y_lo), z: 16, core: 2. Of those that a mesh axis runs over, the one named last changes fastest.
Arguments:
- query_raw: bfloat16 [16, 64, 80, 1536], P('tm', 'height'), may hold values from -40 to 40
- key_raw: bfloat16 [16, 64, 80, 1536], P('tm', 'height'), may hold values from -40 to 40
- values: bfloat16 [16, 64, 80, 1536], P('tm', 'height'), may hold values from -6 to 6
- out_grad: bfloat16 [16, 64, 80, 1536], P('tm', 'height'), may hold values from -6 to 6
- query_gain: float32 [128], replicated, may hold values from 0.5 to 1.5
- key_gain: float32 [128], replicated, may hold values from 0.5 to 1.5
- window: int32 [12, 3], replicated, may hold values from 0 to 2, as said below
Outputs:
- query_grad: bfloat16 [16, 64, 80, 1536], P('tm', 'height')
- key_grad: bfloat16 [16, 64, 80, 1536], P('tm', 'height')
- value_grad: bfloat16 [16, 64, 80, 1536], P('tm', 'height')
- gain_grad: float32 [2, 128], P(None, 'height')
The draws below stay inside these ranges and needn't reach their ends.
Inputs may be any that keep to these rules, and one draw needn't show every extreme that they name: `window`: columns 0 and 1 hold 0 or 1 and column 2 holds 0 to 2; some head has reach (1, 1, 2) and some head (0, 0, 0).
All inputs are finite; a program needn't handle non-finite values.
Results may differ from the reference program's by a relative error of at most 0.008.
Values may be sent and summed in bfloat16 or wider, within the bound.
No kernel may reach another device: no remote copies, remote signals or barrier semaphores. Data moves between devices by JAX's collectives and lax.ppermute only.
A program may use at most 128 MiB of HBM per device.

```python
import math
import jax
import jax.numpy as jnp
from jax import lax

CT = 2
CH = 1
WID = 80
HEADS = 12
HD = 128
TILE_W = 8
WIN_W = 2
FRAMES = 16
ROWS = 64


def draw_query_raw(key, part):
    key = jax.random.fold_in(key, 11)
    key_base, key_scale = jax.random.split(key)
    grid_shape = (FRAMES, ROWS, WID, HEADS, HD)
    scale_shape = (FRAMES, ROWS, WID, HEADS, 1)
    base_rows = jnp.clip(jax.random.normal(key_base, grid_shape, jnp.float32), -4.0, 4.0)
    scales = jnp.exp(jax.random.uniform(key_scale, scale_shape, jnp.float32, 0.0, math.log(10.0)))
    return (base_rows * scales).reshape(FRAMES, ROWS, WID, HEADS * HD).astype(jnp.bfloat16)


def draw_key_raw(key, part):
    key = jax.random.fold_in(key, 12)
    key_base, key_scale = jax.random.split(key)
    grid_shape = (FRAMES, ROWS, WID, HEADS, HD)
    scale_shape = (FRAMES, ROWS, WID, HEADS, 1)
    base_rows = jnp.clip(jax.random.normal(key_base, grid_shape, jnp.float32), -4.0, 4.0)
    scales = jnp.exp(jax.random.uniform(key_scale, scale_shape, jnp.float32, 0.0, math.log(10.0)))
    return (base_rows * scales).reshape(FRAMES, ROWS, WID, HEADS * HD).astype(jnp.bfloat16)


def draw_window(key, part):
    key = jax.random.fold_in(key, 13)
    key_frame, key_row, key_column, key_head = jax.random.split(key, 4)
    reach_frame = jax.random.randint(key_frame, (HEADS,), 0, 2, jnp.int32)
    reach_row = jax.random.randint(key_row, (HEADS,), 0, 2, jnp.int32)
    reach_column = jax.random.randint(key_column, (HEADS,), 0, WIN_W + 1, jnp.int32)
    reach_table = jnp.stack([reach_frame, reach_row, reach_column], axis=1)
    full_head = jax.random.randint(key_head, (), 0, HEADS, jnp.int32)
    head_ids = jnp.arange(HEADS, dtype=jnp.int32)
    widest = jnp.array([1, 1, WIN_W], jnp.int32)
    reach_table = jnp.where((head_ids == full_head)[:, None], widest[None, :], reach_table)
    reach_table = jnp.where((head_ids == (full_head + 1) % HEADS)[:, None], 0, reach_table)
    return reach_table.astype(jnp.int32)


def steps_of(key, extent, shards, smallest, top_value):
    def one(position, blocks):
        draws = jax.random.uniform(jax.random.fold_in(jax.random.fold_in(key, 6), position), (blocks,), jnp.float32, smallest / len(shards), top_value / len(shards))
        return jnp.repeat(jnp.exp(draws), extent[position] // blocks).reshape((-1,) + (1,) * (len(extent) - position - 1))

    level = one(*shards[0])
    for cut in shards[1:]:
        level = level * one(*cut)
    return level


def normal_values(rng, extent, scale, most, pieces=(), kind=jnp.bfloat16):
    values = jax.random.normal(rng, extent, jnp.float32) * scale
    if len(pieces) > 0:
        values = steps_of(rng, extent, pieces, -0.22, 0.18) * values
    return jnp.clip(values, min=-most, max=most).astype(kind)


def setup_inputs(seed: int = 0) -> dict:
    splits = jax.random.split(jax.random.key(seed), 8)
    return {
        "query_raw": draw_query_raw(jax.random.fold_in(splits[7], 71), 0),
        "key_raw": draw_key_raw(jax.random.fold_in(splits[7], 71), 0),
        "values": normal_values(splits[2], (FRAMES, ROWS, WID, HEADS * HD), 1.0, 6.0, ((0, 8), (1, 64))),
        "out_grad": normal_values(splits[3], (FRAMES, ROWS, WID, HEADS * HD), 1.0, 6.0, ((0, 8), (1, 64))),
        "query_gain": jnp.clip(1.0 + 0.1 * jax.random.normal(splits[4], (HD,), jnp.float32), 0.5, 1.5),
        "key_gain": jnp.clip(1.0 + 0.1 * jax.random.normal(splits[5], (HD,), jnp.float32), 0.5, 1.5),
        "window": draw_window(jax.random.fold_in(splits[7], 71), 0),
    }


EPSILON = 1e-06

def normalize(raw_rows, gain_vector):
    full_rows = raw_rows.astype(jnp.float32)
    inverse = lax.rsqrt(lax.optimization_barrier(jnp.mean(full_rows * full_rows, axis=-1, keepdims=True)) + EPSILON)
    unit_rows = full_rows * inverse
    return ((unit_rows * gain_vector).astype(jnp.bfloat16), unit_rows, inverse)

def norm_backward(grad_rows, unit_rows, inverse, gain_vector):
    scaled = grad_rows * gain_vector
    return inverse * (scaled - unit_rows * lax.optimization_barrier(jnp.mean(unit_rows * scaled, axis=-1, keepdims=True)))

def positions(frame_start, row_start, frame_count, row_count, columns):
    frame_ids = frame_start + jnp.arange(frame_count, dtype=jnp.int32)
    row_ids = row_start + jnp.arange(row_count, dtype=jnp.int32)
    column_ids = jnp.arange(columns, dtype=jnp.int32)
    grid_shape = (frame_count, row_count, columns)
    frame_grid = jnp.broadcast_to(frame_ids[:, None, None], grid_shape).reshape(-1)
    row_grid = jnp.broadcast_to(row_ids[None, :, None], grid_shape).reshape(-1)
    column_grid = jnp.broadcast_to(column_ids[None, None, :], grid_shape).reshape(-1)
    return (frame_grid, row_grid, column_grid)

def window_allowed(query_pos, key_pos, key_valid, window):
    frame_gap = jnp.abs(query_pos[0][:, None] - key_pos[0][None, :])
    row_gap = jnp.abs(query_pos[1][:, None] - key_pos[1][None, :])
    tile_gap = jnp.abs(query_pos[2][:, None] // TILE_W - key_pos[2][None, :] // TILE_W)
    return (frame_gap[None] <= window[:, 0, None, None]) & (row_gap[None] <= window[:, 1, None, None]) & (tile_gap[None] <= window[:, 2, None, None]) & key_valid[None, None, :]

def attend(queries, grad_rows, key_rows, value_rows, allowed):
    score_scale = HD ** (-0.5)
    scores = jnp.einsum('qgd,kgd->gqk', queries.astype(jnp.float32), key_rows.astype(jnp.float32)) * score_scale
    weight = jnp.where(allowed, jnp.exp(scores), 0.0)
    row_total = lax.optimization_barrier(jnp.sum(weight, axis=-1, keepdims=True))
    attention = weight / row_total
    prob_back = jnp.einsum('qgd,kgd->gqk', grad_rows.astype(jnp.float32), value_rows.astype(jnp.float32))
    row_delta = lax.optimization_barrier(jnp.sum(attention * prob_back, axis=-1, keepdims=True))
    score_back = lax.optimization_barrier((attention * (prob_back - row_delta) * score_scale).astype(jnp.bfloat16))
    attention_low = lax.optimization_barrier(attention.astype(jnp.bfloat16))
    query_back = jnp.einsum('gqk,kgd->qgd', score_back.astype(jnp.float32), key_rows.astype(jnp.float32))
    key_back = jnp.einsum('gqk,qgd->kgd', score_back.astype(jnp.float32), queries.astype(jnp.float32))
    value_back = jnp.einsum('gqk,qgd->kgd', attention_low.astype(jnp.float32), grad_rows.astype(jnp.float32))
    return (query_back, key_back, value_back)

def reference(query_raw, key_raw, values, out_grad, query_gain, key_gain, window):
    head_shape = (FRAMES, ROWS, WID, HEADS, HD)
    own_count = CT * CH * WID
    ext_count = (CT + 2) * (CH + 2) * WID
    block_rows = ROWS // CH
    block_frames = FRAMES // CT
    key_norm, key_unit, key_inverse = normalize(key_raw.reshape(head_shape), key_gain)
    padding = ((1, 1), (1, 1), (0, 0), (0, 0), (0, 0))
    key_padded = jnp.pad(key_norm, padding)
    value_padded = jnp.pad(values.reshape(head_shape), padding)
    query_heads = query_raw.reshape(head_shape)
    grad_heads = out_grad.reshape(head_shape)
    anchor = jnp.zeros((), jnp.int32)

    def block_step(carried, block_index):
        grad_sum, gain_sum = carried
        frame_start = block_index // block_rows * CT
        row_start = block_index % block_rows * CH
        own_start = (frame_start, row_start, anchor, anchor, anchor)
        own_size = (CT, CH, WID, HEADS, HD)
        ext_size = (CT + 2, CH + 2, WID, HEADS, HD)
        query_slice = lax.dynamic_slice(query_heads, own_start, own_size).reshape(own_count, HEADS, HD)
        grad_slice = lax.dynamic_slice(grad_heads, own_start, own_size).reshape(own_count, HEADS, HD)
        key_slice = lax.dynamic_slice(key_padded, own_start, ext_size).reshape(ext_count, HEADS, HD)
        value_slice = lax.dynamic_slice(value_padded, own_start, ext_size).reshape(ext_count, HEADS, HD)
        query_norm, query_unit, query_inverse = normalize(query_slice, query_gain)
        query_pos = positions(frame_start, row_start, CT, CH, WID)
        key_pos = positions(frame_start - 1, row_start - 1, CT + 2, CH + 2, WID)
        key_valid = (key_pos[0] >= 0) & (key_pos[0] < FRAMES) & (key_pos[1] >= 0) & (key_pos[1] < ROWS)
        allowed = window_allowed(query_pos, key_pos, key_valid, window)
        query_back, key_back, value_back = attend(query_norm, grad_slice, key_slice, value_slice, allowed)
        query_out = norm_backward(query_back, query_unit, query_inverse, query_gain).astype(jnp.bfloat16)
        gain_sum = gain_sum + lax.optimization_barrier(jnp.sum(query_back * query_unit, axis=(0, 1)))
        update = jnp.stack([key_back, value_back]).reshape(2, CT + 2, CH + 2, WID, HEADS, HD)
        sum_start = (anchor, frame_start, row_start, anchor, anchor, anchor)
        current = lax.dynamic_slice(grad_sum, sum_start, update.shape)
        grad_sum = lax.dynamic_update_slice(grad_sum, current + update, sum_start)
        return ((grad_sum, gain_sum), query_out.reshape(CT, CH, WID, HEADS * HD))
    initial = (jnp.zeros((2, FRAMES + 2, ROWS + 2, WID, HEADS, HD), jnp.float32), jnp.zeros((HD,), jnp.float32))
    (grad_sum, query_gain_sum), query_blocks = lax.scan(block_step, initial, jnp.arange(block_frames * block_rows, dtype=jnp.int32))
    query_grad = query_blocks.reshape(block_frames, block_rows, CT, CH, WID, HEADS * HD)
    query_grad = query_grad.transpose(0, 2, 1, 3, 4, 5).reshape(FRAMES, ROWS, WID, HEADS * HD)
    key_back = grad_sum[0, 1:-1, 1:-1]
    value_grad = grad_sum[1, 1:-1, 1:-1].astype(jnp.bfloat16).reshape(FRAMES, ROWS, WID, HEADS * HD)
    key_grad = norm_backward(key_back, key_unit, key_inverse, key_gain).astype(jnp.bfloat16).reshape(FRAMES, ROWS, WID, HEADS * HD)
    key_gain_sum = lax.optimization_barrier(jnp.sum(key_back * key_unit, axis=(0, 1, 2, 3)))
    gain_grad = jnp.stack([query_gain_sum, key_gain_sum])
    return (query_grad, key_grad, value_grad, gain_grad)
```

```python
import functools

import jax
import jax.numpy as jnp
from jax import lax
from jax.experimental import pallas as pl
from jax.experimental.pallas import tpu as pltpu
from jax.sharding import PartitionSpec as P

TILE_W = 8
EPSILON = 1e-06
HEAD_DIM = 128
LOG2E = 1.4426950408889634
BLOCKED = 1000.0
LANES = 128
BOTH = ("tm", "height")


def rms_inverse(full_rows):
    return lax.rsqrt(jnp.mean(full_rows * full_rows, axis=-1, keepdims=True) + EPSILON)


def norm_backward(grad_rows, unit_rows, inverse, gain_row):
    scaled = grad_rows * gain_row
    return inverse * (scaled - unit_rows * jnp.mean(unit_rows * scaled, axis=-1, keepdims=True))


def pack_kernel(key_ref, value_ref, gain_ref, both_ref, first_ref, last_ref):
    frames, width, _ = key_ref.shape
    gain_row = gain_ref[...]
    edges = (first_ref, last_ref)
    for f in range(frames):
        full_rows = key_ref[f].astype(jnp.float32)
        key_rows = (full_rows * rms_inverse(full_rows) * gain_row).astype(jnp.bfloat16)
        both_ref[f, 0] = key_rows
        both_ref[f, 1] = value_ref[f]
        edges[f][0] = key_rows
        edges[f][1] = value_ref[f]


def head_block(lead):
    zeros = (0,) * len(lead)
    return pl.BlockSpec((*lead, LANES), lambda g: (*zeros, g))


def fixed_block(shape):
    zeros = (0,) * len(shape)
    return pl.BlockSpec(shape, lambda g: zeros)


def smem_block():
    return pl.BlockSpec(memory_space=pltpu.SMEM)


def pack(key_raw, values, key_gain):
    frames, width, channels = key_raw.shape
    heads = channels // LANES
    kinds = jax.ShapeDtypeStruct
    return pl.pallas_call(
        pack_kernel,
        grid=(heads,),
        in_specs=[head_block((frames, width)), head_block((frames, width)), fixed_block((1, LANES))],
        out_specs=[head_block((frames, 2, width)), head_block((2, width)), head_block((2, width))],
        out_shape=[
            kinds((frames, 2, width, channels), jnp.bfloat16),
            kinds((2, width, channels), jnp.bfloat16),
            kinds((2, width, channels), jnp.bfloat16),
        ],
        name="pack_keys_values",
    )(key_raw, values, key_gain)


def padded(count):
    return -(-count // LANES) * LANES


def variants():
    out = {}
    for rows_on in (0, 1):
        for frames_on in (0, 1):
            rows = (0, 1, 2) if rows_on else (0,)
            frames = (0, 1, 2, 3) if frames_on else (1, 2)
            out[rows_on, frames_on] = [(r, e) for r in rows for e in frames]
    return out


def fill_distance(dist_ref, blocks, width, valid_ref):
    queries, keys = dist_ref.shape
    q_ids = lax.broadcasted_iota(jnp.int32, (queries, keys), 0)
    k_ids = lax.broadcasted_iota(jnp.int32, (queries, keys), 1)
    q_frame = (q_ids >= width).astype(jnp.int32)
    q_tile = (q_ids - q_frame * width) // TILE_W
    k_block = jnp.zeros_like(k_ids)
    for i in range(1, len(blocks) + 1):
        k_block += (k_ids >= i * width).astype(jnp.int32)
    k_tile = (k_ids - k_block * width) // TILE_W
    gap = jnp.abs(q_tile - k_tile).astype(jnp.float32)
    reach = 1 if any(e == 0 for _, e in blocks) else 0
    allowed = jnp.zeros((queries, keys), jnp.float32)
    for i, (r, e) in enumerate(blocks):
        here = jnp.logical_and(k_block == i, jnp.abs(q_frame + 1 - e) <= reach)
        ok = jnp.float32(1.0)
        if r == 2:
            ok = ok * valid_ref[0].astype(jnp.float32)
        if e == 0:
            ok = ok * valid_ref[1].astype(jnp.float32)
        if e == 3:
            ok = ok * valid_ref[2].astype(jnp.float32)
        allowed += jnp.where(here, ok, 0.0)
    dist_ref[...] = jnp.where(allowed > 0.5, gap, BLOCKED)


def matmul(a, b, dims):
    return lax.dot_general(a, b, (dims, ((), ())), preferred_element_type=jnp.float32)


def attend_kernel(
    window_ref, valid_ref, query_ref, grad_ref, own_ref, chip_ref, off_ref,
    prev_ref, next_ref, chip_prev_ref, chip_next_ref, off_prev_ref, off_next_ref,
    q_gain_ref, k_gain_ref,
    query_grad_ref, own_out, chip_out, off_out,
    prev_out, next_out, chip_prev_out, chip_next_out, off_prev_out, off_next_out, gain_out,
    key_buf, value_buf, *dist_refs,
):
    step = pl.program_id(0)
    frames, width, head_dim = query_ref.shape
    tokens = frames * width
    table = variants()
    dists = dict(zip(table, dist_refs))
    scale = head_dim ** (-0.5)

    sources = {}
    targets = {}
    rows_in = ((own_ref, prev_ref, next_ref), (chip_ref, chip_prev_ref, chip_next_ref), (off_ref, off_prev_ref, off_next_ref))
    rows_out = ((own_out, prev_out, next_out), (chip_out, chip_prev_out, chip_next_out), (off_out, off_prev_out, off_next_out))
    for r in range(3):
        for refs, where in ((rows_in[r], sources), (rows_out[r], targets)):
            where[r, 0] = refs[1]
            where[r, 1] = refs[0].at[0]
            where[r, 2] = refs[0].at[1]
            where[r, 3] = refs[2]

    @pl.when(step == 0)
    def _():
        key_buf[...] = jnp.zeros_like(key_buf)
        value_buf[...] = jnp.zeros_like(value_buf)
        gain_out[...] = jnp.zeros_like(gain_out)
        for which, blocks in table.items():
            fill_distance(dists[which], blocks, width, valid_ref)

    frame_reach = window_ref[step, 0]
    row_reach = window_ref[step, 1]
    tile_reach = window_ref[step, 2].astype(jnp.float32)

    def work(which):
        blocks = table[which]
        keys = padded(len(blocks) * width)
        for i, block in enumerate(blocks):
            key_buf[i * width : (i + 1) * width] = sources[block][0]
            value_buf[i * width : (i + 1) * width] = sources[block][1]
        gain_row = q_gain_ref[...]
        full_rows = query_ref[...].reshape(tokens, head_dim).astype(jnp.float32)
        inverse = rms_inverse(full_rows)
        unit_rows = full_rows * inverse
        queries = (unit_rows * gain_row).astype(jnp.bfloat16)
        grads = grad_ref[...].reshape(tokens, head_dim)
        key_rows = key_buf[0:keys]
        value_rows = value_buf[0:keys]
        scores = matmul(queries, key_rows, ((1,), (1,)))
        weight = jnp.where(
            dists[which][...] <= tile_reach, jnp.exp2(scores * (scale * LOG2E)), 0.0
        )
        total = jnp.sum(weight, axis=-1, keepdims=True)
        prob = weight * (1.0 / total)
        prob_back = matmul(grads, value_rows, ((1,), (1,)))
        delta = jnp.sum(prob * prob_back, axis=-1, keepdims=True)
        score_back = (prob * ((prob_back - delta) * scale)).astype(jnp.bfloat16)
        query_back = matmul(score_back, key_rows, ((1,), (0,)))
        key_back = matmul(score_back, queries, ((0,), (0,)))
        value_back = matmul(prob.astype(jnp.bfloat16), grads, ((0,), (0,)))
        for i, block in enumerate(blocks):
            out = targets[block]
            out[0] = key_back[i * width : (i + 1) * width].astype(out.dtype)
            out[1] = value_back[i * width : (i + 1) * width].astype(out.dtype)
        for block, out in targets.items():
            if block not in blocks:
                out[...] = jnp.zeros_like(out)
        result = norm_backward(query_back, unit_rows, inverse, gain_row)
        query_grad_ref[...] = result.reshape(frames, width, head_dim).astype(query_grad_ref.dtype)
        gain_out[0:1] += jnp.sum(query_back * unit_rows, axis=0, keepdims=True)
        gain_out[1:2] += jnp.sum(query_back * queries.astype(jnp.float32), axis=0, keepdims=True) / k_gain_ref[...]

    for which in table:
        rows_on, frames_on = which

        @pl.when(jnp.logical_and(row_reach == rows_on, frame_reach == frames_on))
        def _(which=which):
            work(which)


def attend(window, valid, query_raw, out_grad, own, chip, off, edges, query_gain, key_gain):
    frames, width, channels = query_raw.shape
    heads = channels // LANES
    kinds = jax.ShapeDtypeStruct
    token = head_block((frames, width))
    pair = head_block((frames, 2, width))
    edge = head_block((2, width))
    gain = fixed_block((1, LANES))
    pair_shape = (frames, 2, width, channels)
    edge_shape = (2, width, channels)
    most = padded(12 * width)
    return pl.pallas_call(
        attend_kernel,
        grid=(heads,),
        in_specs=[smem_block(), smem_block(), token, token, pair, pair, pair] + [edge] * 6 + [gain, gain],
        out_specs=[token, pair, pair, pair] + [edge] * 6 + [fixed_block((2, LANES))],
        out_shape=[
            kinds(query_raw.shape, jnp.bfloat16),
            kinds(pair_shape, jnp.float32),
            kinds(pair_shape, jnp.bfloat16),
            kinds(pair_shape, jnp.bfloat16),
        ]
        + [kinds(edge_shape, jnp.bfloat16)] * 6
        + [kinds((2, LANES), jnp.float32)],
        scratch_shapes=[
            pltpu.VMEM((most, LANES), jnp.bfloat16),
            pltpu.VMEM((most, LANES), jnp.bfloat16),
        ]
        + [
            pltpu.VMEM((frames * width, padded(len(blocks) * width)), jnp.float32)
            for blocks in variants().values()
        ],
        compiler_params=pltpu.CompilerParams(vmem_limit_bytes=40 * 1024 * 1024),
        name="attend",
    )(window, valid, query_raw, out_grad, own, chip, off, *edges, query_gain, key_gain)


def finish_kernel(
    key_ref, own_ref, chip_ref, off_ref, first_ref, last_ref, off_first_ref, off_last_ref, gain_ref,
    key_grad_ref, value_grad_ref,
):
    frames = key_ref.shape[0]
    gain_row = gain_ref[...]
    edges = ((first_ref, off_first_ref), (last_ref, off_last_ref))
    for f in range(frames):
        sums = []
        for c in range(2):
            terms = own_ref[f, c]
            for ref in (chip_ref.at[f], off_ref.at[f], *edges[f]):
                terms = terms + ref[c].astype(jnp.float32)
            sums.append(terms)
        full_rows = key_ref[f].astype(jnp.float32)
        inverse = rms_inverse(full_rows)
        result = norm_backward(sums[0], full_rows * inverse, inverse, gain_row)
        key_grad_ref[f] = result.astype(key_grad_ref.dtype)
        value_grad_ref[f] = sums[1].astype(value_grad_ref.dtype)


def finish(key_raw, own, chip, off, edges, key_gain):
    frames, width, channels = key_raw.shape
    heads = channels // LANES
    token = head_block((frames, width))
    pair = head_block((frames, 2, width))
    edge = head_block((2, width))
    return pl.pallas_call(
        finish_kernel,
        grid=(heads,),
        in_specs=[token, pair, pair, pair] + [edge] * 4 + [fixed_block((1, LANES))],
        out_specs=[token, token],
        out_shape=[jax.ShapeDtypeStruct(key_raw.shape, jnp.bfloat16)] * 2,
        name="finish_keys",
    )(key_raw, own, chip, off, *edges, key_gain)


def off_chip(h):
    return h + 1 if h % 2 else h - 1


def move(block, frame_step, row_rule):
    frames_size, rows_size = lax.axis_size("tm"), lax.axis_size("height")
    route = []
    for t in range(frames_size):
        for h in range(rows_size):
            to_t, to_h = t + frame_step, row_rule(h)
            if 0 <= to_t < frames_size and 0 <= to_h < rows_size:
                route.append((t * rows_size + h, to_t * rows_size + to_h))
    return lax.ppermute(block, BOTH, route)


def same_row(h):
    return h


def chip_row(h):
    return h ^ 1


def on_device(query_raw, key_raw, values, out_grad, query_gain, key_gain, window):
    frames, _, width, channels = query_raw.shape
    flat = (frames, width, channels)
    t, h = lax.axis_index("tm"), lax.axis_index("height")
    t_size, h_size = lax.axis_size("tm"), lax.axis_size("height")
    partner = jnp.where(h % 2 == 1, h + 1, h - 1)
    valid = jnp.stack(
        [jnp.logical_and(partner >= 0, partner < h_size), t > 0, t < t_size - 1]
    ).astype(jnp.int32)
    q_gain, k_gain = query_gain[None], key_gain[None]
    key_flat = key_raw.reshape(flat)
    own, first, last = pack(key_flat, values.reshape(flat), k_gain)

    prev = move(last, 1, same_row)
    following = move(first, -1, same_row)
    off = move(own, 0, off_chip)
    chip = move(own, 0, chip_row)
    off_prev = move(last, 1, off_chip)
    off_next = move(first, -1, off_chip)
    chip_prev = move(prev, 0, chip_row)
    chip_next = move(following, 0, chip_row)

    (
        query_grad, own_sum, chip_sum, off_sum,
        prev_sum, next_sum, chip_prev_sum, chip_next_sum, off_prev_sum, off_next_sum, gain_part,
    ) = attend(
        window, valid, query_raw.reshape(flat), out_grad.reshape(flat), own, chip, off,
        (prev, following, chip_prev, chip_next, off_prev, off_next), q_gain, k_gain,
    )

    def add(a, b):
        return (a.astype(jnp.float32) + b.astype(jnp.float32)).astype(jnp.bfloat16)

    prev_all = add(prev_sum, move(chip_prev_sum, 0, chip_row))
    next_all = add(next_sum, move(chip_next_sum, 0, chip_row))
    off_back = move(off_sum, 0, off_chip)
    last_back = move(prev_all, -1, same_row)
    first_back = move(next_all, 1, same_row)
    off_last_back = move(off_prev_sum, -1, off_chip)
    off_first_back = move(off_next_sum, 1, off_chip)
    chip_back = move(chip_sum, 0, chip_row)

    per_row = LANES // h_size
    pieces = gain_part.reshape(2, h_size, per_row).transpose(1, 0, 2).reshape(1, h_size, 2 * per_row)
    pieces = jnp.broadcast_to(pieces, (t_size, h_size, 2 * per_row)).reshape(t_size * h_size, 2 * per_row)
    gain_grad = lax.all_to_all(pieces, BOTH, 0, 0, tiled=True).sum(0).reshape(2, per_row)

    key_grad, value_grad = finish(
        key_flat, own_sum, chip_back, off_back, (first_back, last_back, off_first_back, off_last_back), k_gain
    )
    shape = query_raw.shape
    return (query_grad.reshape(shape), key_grad.reshape(shape), value_grad.reshape(shape), gain_grad)


def solution(mesh):
    token = P("tm", "height", None, None)
    return jax.shard_map(
        on_device,
        mesh=mesh,
        in_specs=(token, token, token, token, P(), P(), P()),
        out_specs=(token, token, token, P(None, "height")),
        check_vma=False,
    )
```

```python
import functools

import jax
import jax.numpy as jnp
from jax import lax
from jax.experimental import pallas as pl
from jax.experimental.pallas import tpu as pltpu
from jax.sharding import PartitionSpec as P

TILE_W = 8
EPSILON = 1e-06
HEAD_DIM = 128
LOG2E = 1.4426950408889634
BLOCKED = 1000.0
LANES = 128
BOTH = ("tm", "height")
SIZES = [(6, 6, 4), (7, 7, 5), (8, 8, 6)]
VMEM_BYTES = 56 * 1024 * 1024


def rms_inverse(full_rows):
    return lax.rsqrt(jnp.mean(full_rows * full_rows, axis=-1, keepdims=True) + EPSILON)


def norm_backward(grad_rows, unit_rows, inverse, gain_row):
    scaled = grad_rows * gain_row
    return inverse * (scaled - unit_rows * jnp.mean(unit_rows * scaled, axis=-1, keepdims=True))


def whole(memory_space=pltpu.VMEM):
    return pl.BlockSpec(memory_space=memory_space)


def params():
    return pltpu.CompilerParams(vmem_limit_bytes=VMEM_BYTES)


def head_lanes(g):
    return pl.ds(pl.multiple_of(g * LANES, LANES), LANES)


def pack_kernel(
    window_ref, key_ref, value_ref, gain_ref,
    slots_ref, own_ref, row_ref, first_ref, last_ref, corner_first_ref, corner_last_ref,
):
    frames, width, channels = key_ref.shape
    gain_row = gain_ref[...]
    edges = ((first_ref, corner_first_ref), (last_ref, corner_last_ref))

    def one_head(g, counts):
        lanes = head_lanes(g)
        row_on, frame_on = window_ref[g, 1], window_ref[g, 0]
        counts = tuple(c + on for c, on in zip(counts, (row_on, frame_on, row_on * frame_on)))
        slots = [jnp.maximum(c - 1, 0) for c in counts]
        for kind in range(3):
            slots_ref[kind, g] = slots[kind]
        pairs = []
        for f in range(frames):
            full_rows = key_ref[f, :, lanes].astype(jnp.float32)
            pairs.append(
                ((full_rows * rms_inverse(full_rows) * gain_row).astype(jnp.bfloat16), value_ref[f, :, lanes])
            )
            for c in range(2):
                own_ref[f, c, :, lanes] = pairs[f][c]

        @pl.when(row_on == 1)
        def _():
            for f in range(frames):
                for c in range(2):
                    row_ref[slots[0], f, c] = pairs[f][c]

        @pl.when(frame_on == 1)
        def _():
            for f in range(frames):
                for c in range(2):
                    edges[f][0][slots[1], c] = pairs[f][c]

        @pl.when(row_on * frame_on == 1)
        def _():
            for f in range(frames):
                for c in range(2):
                    edges[f][1][slots[2], c] = pairs[f][c]

        return counts

    zero = jnp.int32(0)
    lax.fori_loop(0, channels // LANES, one_head, (zero, zero, zero))


def pack(window, key_raw, values, key_gain, sizes):
    frames, width, channels = key_raw.shape
    kinds = jax.ShapeDtypeStruct
    low = jnp.bfloat16
    shapes = [(frames, 2, width, channels), (sizes[0], frames, 2, width, LANES)]
    shapes += [(sizes[1], 2, width, LANES)] * 2 + [(sizes[2], 2, width, LANES)] * 2
    return pl.pallas_call(
        pack_kernel,
        in_specs=[whole(pltpu.SMEM)] + [whole()] * 3,
        out_specs=[whole(pltpu.SMEM)] + [whole()] * 6,
        out_shape=[kinds((3, channels // LANES), jnp.int32)] + [kinds(shape, low) for shape in shapes],
        compiler_params=params(),
        name="pack_keys_values",
    )(window, key_raw, values, key_gain)


def matmul(a, b, dims):
    return lax.dot_general(a, b, (dims, ((), ())), preferred_element_type=jnp.float32)


def attend_kernel(
    window_ref, slots_ref, query_ref, grad_ref, own_ref, chip_ref, off_ref,
    prev_ref, next_ref, chip_prev_ref, chip_next_ref, off_prev_ref, off_next_ref,
    q_gain_ref, k_gain_ref,
    query_grad_ref, own_out, chip_out, off_out, prev_out, next_out, gain_out,
    key_buf, value_buf, key_sum, value_sum, gap_ref,
):
    frames, width, _ = query_ref.shape
    head_dim = LANES
    scale = head_dim ** (-0.5)

    key_buf[...] = jnp.zeros_like(key_buf)
    value_buf[...] = jnp.zeros_like(value_buf)
    gain_out[...] = jnp.zeros_like(gain_out)
    q_ids = lax.broadcasted_iota(jnp.int32, gap_ref.shape, 0)
    k_ids = lax.broadcasted_iota(jnp.int32, gap_ref.shape, 1)
    gap_ref[...] = jnp.abs(q_ids // TILE_W - k_ids % width // TILE_W).astype(jnp.float32)
    gain_row = q_gain_ref[...]
    full, part = span_sizes(width)
    t, h = lax.axis_index("tm"), lax.axis_index("height")
    has_off = jnp.logical_and(h > 0, h < lax.axis_size("height") - 1).astype(jnp.int32)
    has_prev = (t > 0).astype(jnp.int32)
    has_next = (t < lax.axis_size("tm") - 1).astype(jnp.int32)

    def one_head(g, carry):
        frame_reach = window_ref[g, 0]
        row_reach = window_ref[g, 1]
        tile_reach = window_ref[g, 2].astype(jnp.float32)
        row_count = 1 + 2 * row_reach
        lanes = head_lanes(g)
        row_slot, frame_slot, corner_slot = slots_ref[0, g], slots_ref[1, g], slots_ref[2, g]

        def place(r, e):
            return pl.ds(pl.multiple_of((e * row_count + r) * width, 16), width)

        def load(r, e, ref):
            key_buf[place(r, e)] = ref[0]
            value_buf[place(r, e)] = ref[1]

        def store(r, e, ref):
            ref[0] = key_sum[place(r, e)].astype(ref.dtype)
            ref[1] = value_sum[place(r, e)].astype(ref.dtype)

        def each_block(do, own, prev, following, chip, off, corners):
            for f in range(frames):
                do(0, f + 1, own[f])

            @pl.when(frame_reach == 1)
            def _():
                do(0, 0, prev)
                do(0, frames + 1, following)

            @pl.when(row_reach == 1)
            def _():
                for f in range(frames):
                    do(1, f + 1, chip[f])
                    do(2, f + 1, off[f])

            @pl.when(frame_reach * row_reach == 1)
            def _():
                for r in range(2):
                    do(r + 1, 0, corners[r][0])
                    do(r + 1, frames + 1, corners[r][1])

        each_block(
            load, [own_ref.at[f, :, :, lanes] for f in range(frames)], prev_ref.at[frame_slot], next_ref.at[frame_slot],
            [chip_ref.at[row_slot, f] for f in range(frames)], [off_ref.at[row_slot, f] for f in range(frames)],
            (
                (chip_prev_ref.at[frame_slot], chip_next_ref.at[frame_slot]),
                (off_prev_ref.at[corner_slot], off_next_ref.at[corner_slot]),
            ),
        )
        key_sum[...] = jnp.zeros_like(key_sum)
        value_sum[...] = jnp.zeros_like(value_sum)

        def work(keys):
            both = range(frames)
            k_block = lax.broadcasted_iota(jnp.int32, (1, keys), 1) // width
            frame = k_block // row_count
            row = k_block - frame * row_count
            gap = gap_ref[:, 0:keys]
            spans, unit, inverse, queries, grads, scores, prob_back, inside = [], [], [], [], [], [], [], []
            for f in both:
                start = (f + 1 - frame_reach) * row_count * width
                spans.append(pl.ds(pl.multiple_of(start, 16), keys))
                ext = f + 1 - frame_reach + frame
                shut = frame > 2 * frame_reach
                shut = jnp.logical_or(shut, jnp.logical_and(row == 2, has_off == 0))
                shut = jnp.logical_or(shut, jnp.logical_and(ext == 0, has_prev == 0))
                shut = jnp.logical_or(shut, jnp.logical_and(ext == frames + 1, has_next == 0))
                inside.append(gap + jnp.where(shut, BLOCKED, 0.0) <= tile_reach)
                full_rows = query_ref[f, :, lanes].astype(jnp.float32)
                inverse.append(rms_inverse(full_rows))
                unit.append(full_rows * inverse[f])
                queries.append((unit[f] * gain_row).astype(jnp.bfloat16))
                grads.append(grad_ref[f, :, lanes])
            for f in both:
                scores.append(matmul(queries[f], key_buf[spans[f]], ((1,), (1,))))
                prob_back.append(matmul(grads[f], value_buf[spans[f]], ((1,), (1,))))
            weight = [jnp.where(inside[f], jnp.exp2(scores[f] * (scale * LOG2E)), 0.0) for f in both]
            total = [jnp.sum(w, axis=-1, keepdims=True) for w in weight]
            inner = [jnp.sum(weight[f] * prob_back[f], axis=-1, keepdims=True) for f in both]
            over = [1.0 / x for x in total]
            prob = [weight[f] * over[f] for f in both]
            delta = [inner[f] * over[f] for f in both]
            score_back = [(prob[f] * ((prob_back[f] - delta[f]) * scale)).astype(jnp.bfloat16) for f in both]
            low = [p.astype(jnp.bfloat16) for p in prob]
            query_back = [matmul(score_back[f], key_buf[spans[f]], ((1,), (0,))) for f in both]
            key_back = [matmul(score_back[f], queries[f], ((0,), (0,))) for f in both]
            value_back = [matmul(low[f], grads[f], ((0,), (0,))) for f in both]
            for f in both:
                key_sum[spans[f]] += key_back[f]
                value_sum[spans[f]] += value_back[f]
                result = norm_backward(query_back[f], unit[f], inverse[f], gain_row)
                query_grad_ref[f, :, lanes] = result.astype(query_grad_ref.dtype)
            first = sum(jnp.sum(query_back[f] * unit[f], axis=0, keepdims=True) for f in both)
            second = sum(jnp.sum(query_back[f] * queries[f].astype(jnp.float32), axis=0, keepdims=True) for f in both)
            gain_out[0:1] += first
            gain_out[1:2] += second / k_gain_ref[...]

        wide = frame_reach * row_reach == 1
        pl.when(wide)(lambda: work(full))
        pl.when(jnp.logical_not(wide))(lambda: work(part))

        each_block(
            store, [own_out.at[g, f] for f in range(frames)], prev_out.at[frame_slot], next_out.at[frame_slot],
            [chip_out.at[row_slot, f + 1] for f in range(frames)], [off_out.at[row_slot, f + 1] for f in range(frames)],
            tuple((out.at[row_slot, 0], out.at[row_slot, frames + 1]) for out in (chip_out, off_out)),
        )
        return carry

    lax.fori_loop(0, window_ref.shape[0], one_head, 0)


def span_sizes(width):
    return tuple(-(-blocks * width // LANES) * LANES for blocks in (9, 3))


def attend(window, slots, query_raw, out_grad, own, chip, off, edges, corners, query_gain, key_gain):
    frames, width, channels = query_raw.shape
    heads = channels // LANES
    kinds = jax.ShapeDtypeStruct
    sent_shape = (chip.shape[0], frames + 2, 2, width, LANES)
    edge_shape = edges[0].shape
    most = 3 * width + span_sizes(width)[0]
    return pl.pallas_call(
        attend_kernel,
        in_specs=[whole(pltpu.SMEM)] * 2 + [whole()] * 13,
        out_specs=[whole()] * 7,
        out_shape=[
            kinds(query_raw.shape, jnp.bfloat16),
            kinds((heads, frames, 2, width, LANES), jnp.float32),
            kinds(sent_shape, jnp.bfloat16),
            kinds(sent_shape, jnp.bfloat16),
            kinds(edge_shape, jnp.float32),
            kinds(edge_shape, jnp.float32),
            kinds((2, LANES), jnp.float32),
        ],
        scratch_shapes=[
            pltpu.VMEM((most, LANES), jnp.bfloat16),
            pltpu.VMEM((most, LANES), jnp.bfloat16),
            pltpu.VMEM((most, LANES), jnp.float32),
            pltpu.VMEM((most, LANES), jnp.float32),
            pltpu.VMEM((width, span_sizes(width)[0]), jnp.float32),
        ],
        compiler_params=params(),
        name="attend",
    )(window, slots, query_raw, out_grad, own, chip, off, *edges, *corners, query_gain, key_gain)


def relay_kernel(window_ref, slots_ref, prev_ref, next_ref, chip_ref, off_ref, prev_out, next_out):
    last = chip_ref.shape[1] - 1

    def one_head(g, carry):
        row_on, frame_on = window_ref[g, 1], window_ref[g, 0]
        row_slot, frame_slot = slots_ref[0, g], slots_ref[1, g]

        @pl.when(jnp.logical_and(frame_on == 1, row_on == 0))
        def _():
            for kept, out in ((prev_ref, prev_out), (next_ref, next_out)):
                out[frame_slot] = kept[frame_slot].astype(out.dtype)

        @pl.when(jnp.logical_and(frame_on == 1, row_on == 1))
        def _():
            for kept, out, e in ((prev_ref, prev_out, 0), (next_ref, next_out, last)):
                terms = kept[frame_slot] + chip_ref[row_slot, e].astype(jnp.float32)
                out[frame_slot] = (terms + off_ref[row_slot, e].astype(jnp.float32)).astype(out.dtype)

        return carry

    lax.fori_loop(0, window_ref.shape[0], one_head, 0)


def relay(window, slots, kept, chip, off):
    return pl.pallas_call(
        relay_kernel,
        in_specs=[whole(pltpu.SMEM)] * 2 + [whole()] * 4,
        out_specs=[whole()] * 2,
        out_shape=[jax.ShapeDtypeStruct(kept[0].shape, jnp.bfloat16)] * 2,
        compiler_params=params(),
        name="add_corner_terms",
    )(window, slots, *kept, chip, off)


def finish_kernel(
    window_ref, slots_ref, key_ref, own_ref, chip_ref, off_ref, first_ref, last_ref, gain_ref,
    key_grad_ref, value_grad_ref,
):
    frames = key_ref.shape[0]
    gain_row = gain_ref[...]
    edges = (first_ref, last_ref)

    def one_head(g, carry):
        lanes = head_lanes(g)
        row_on, frame_on = window_ref[g, 1] == 1, window_ref[g, 0] == 1
        row_slot, frame_slot = slots_ref[0, g], slots_ref[1, g]
        for f in range(frames):
            sums = []
            for c in range(2):
                rows = chip_ref[row_slot, f + 1, c].astype(jnp.float32) + off_ref[row_slot, f + 1, c].astype(jnp.float32)
                edge = edges[f][frame_slot, c].astype(jnp.float32)
                sums.append(own_ref[g, f, c] + jnp.where(row_on, rows, 0.0) + jnp.where(frame_on, edge, 0.0))
            full_rows = key_ref[f, :, lanes].astype(jnp.float32)
            inverse = rms_inverse(full_rows)
            result = norm_backward(sums[0], full_rows * inverse, inverse, gain_row)
            key_grad_ref[f, :, lanes] = result.astype(key_grad_ref.dtype)
            value_grad_ref[f, :, lanes] = sums[1].astype(value_grad_ref.dtype)
        return carry

    lax.fori_loop(0, window_ref.shape[0], one_head, 0, unroll=2)


def finish(window, slots, key_raw, own, chip, off, edges, key_gain):
    frames, width, _ = key_raw.shape
    return pl.pallas_call(
        finish_kernel,
        in_specs=[whole(pltpu.SMEM)] * 2 + [whole()] * 7,
        out_specs=[whole()] * 2,
        out_shape=[jax.ShapeDtypeStruct(key_raw.shape, jnp.bfloat16)] * 2,
        compiler_params=params(),
        name="finish_keys",
    )(window, slots, key_raw, own, chip, off, *edges, key_gain)


def off_chip(h):
    return h + 1 if h % 2 else h - 1


def move(block, frame_step, row_rule):
    frames_size, rows_size = lax.axis_size("tm"), lax.axis_size("height")
    route = []
    for t in range(frames_size):
        for h in range(rows_size):
            to_t, to_h = t + frame_step, row_rule(h)
            if 0 <= to_t < frames_size and 0 <= to_h < rows_size:
                route.append((t * rows_size + h, to_t * rows_size + to_h))
    return lax.ppermute(block, BOTH, route)


def same_row(h):
    return h


def chip_row(h):
    return h ^ 1


def sum_over_rows(part):
    rows_size = lax.axis_size("height")
    per_row = LANES // rows_size
    pieces = part.reshape(2, rows_size, per_row).transpose(1, 0, 2).reshape(rows_size, 2 * per_row)
    return lax.all_to_all(pieces, "height", 0, 0, tiled=True).sum(0, keepdims=True)


def sum_over_frames(mine):
    copies = jnp.broadcast_to(mine, (lax.axis_size("tm"), mine.shape[1]))
    return lax.all_to_all(copies, "tm", 0, 0, tiled=True).sum(0).reshape(2, mine.shape[1] // 2)


def with_sizes(sizes, query_flat, key_flat, value_flat, grad_flat, q_gain, k_gain, window):
    slots, own, rows, first, last, corner_first, corner_last = pack(window, key_flat, value_flat, k_gain, sizes)
    off = move(rows, 0, off_chip)
    prev = move(last, 1, same_row)
    following = move(first, -1, same_row)
    off_prev = move(corner_last, 1, off_chip)
    off_next = move(corner_first, -1, off_chip)
    rows, prev, following, off_prev, off_next = lax.optimization_barrier((rows, prev, following, off_prev, off_next))
    chip = move(rows, 0, chip_row)
    chip_prev = move(prev, 0, chip_row)
    chip_next = move(following, 0, chip_row)

    query_grad, own_sum, chip_sum, off_sum, prev_sum, next_sum, gain_part = attend(
        window, slots, query_flat, grad_flat, own, chip, off,
        (prev, following, chip_prev, chip_next), (off_prev, off_next), q_gain, k_gain,
    )

    off_back = move(off_sum, 0, off_chip)
    chip_back = move(chip_sum, 0, chip_row)
    mine = sum_over_rows(gain_part)
    chip_back, off_back, mine = lax.optimization_barrier((chip_back, off_back, mine))
    prev_all, next_all = relay(window, slots, (prev_sum, next_sum), chip_back, off_back)
    last_back = move(prev_all, -1, same_row)
    first_back = move(next_all, 1, same_row)
    gain_grad = sum_over_frames(mine)
    first_back, last_back, gain_grad = lax.optimization_barrier((first_back, last_back, gain_grad))
    key_grad, value_grad = finish(
        window, slots, key_flat, own_sum, chip_back, off_back, (first_back, last_back), k_gain
    )
    return query_grad, key_grad, value_grad, gain_grad


def on_device(query_raw, key_raw, values, out_grad, query_gain, key_gain, window):
    frames, _, width, channels = query_raw.shape
    heads = channels // LANES
    flat = (frames, width, channels)
    row_on, frame_on = window[:, 1], window[:, 0]
    row_count, frame_count, both_count = jnp.sum(row_on), jnp.sum(frame_on), jnp.sum(row_on * frame_on)
    choices = SIZES + [(heads, heads, heads)]
    choice = jnp.int32(0)
    for sizes in SIZES:
        fits = (row_count <= sizes[0]) & (frame_count <= sizes[1]) & (both_count <= sizes[2])
        choice += 1 - fits.astype(jnp.int32)
    args = [x.reshape(flat) for x in (query_raw, key_raw, values, out_grad)]
    outs = lax.switch(
        choice,
        [functools.partial(with_sizes, sizes) for sizes in choices],
        *args, query_gain[None], key_gain[None], window,
    )
    return tuple(x.reshape(query_raw.shape) for x in outs[:3]) + (outs[3],)


def solution(mesh):
    token = P("tm", "height", None, None)
    return jax.shard_map(
        on_device,
        mesh=mesh,
        in_specs=(token, token, token, token, P(), P(), P()),
        out_specs=(token, token, token, P(None, "height")),
        check_vma=False,
    )
```

```python
import functools

import jax
import jax.numpy as jnp
from jax import lax
from jax.experimental import pallas as pl
from jax.experimental.pallas import tpu as pltpu
from jax.sharding import PartitionSpec as P

TILE_W = 8
EPSILON = 1e-06
HEAD_DIM = 128
LOG2E = 1.4426950408889634
BLOCKED = 1000.0
LANES = 128
BOTH = ("tm", "height")
SIZES = [(6, 6, 4), (8, 8, 6), (10, 10, 8)]
GROUP = 3
VMEM_BYTES = 56 * 1024 * 1024


def rms_inverse(full_rows):
    return lax.rsqrt(jnp.mean(full_rows * full_rows, axis=-1, keepdims=True) + EPSILON)


def norm_backward(grad_rows, unit_rows, inverse, gain_row):
    scaled = grad_rows * gain_row
    return inverse * (scaled - unit_rows * jnp.mean(unit_rows * scaled, axis=-1, keepdims=True))


def whole(memory_space=pltpu.VMEM):
    return pl.BlockSpec(memory_space=memory_space)


def params():
    return pltpu.CompilerParams(vmem_limit_bytes=VMEM_BYTES)


def head_lanes(g):
    return pl.ds(pl.multiple_of(g * LANES, LANES), LANES)


def pack_kernel(
    window_ref, key_ref, value_ref, gain_ref,
    slots_ref, own_ref, row_ref, first_ref, last_ref, corner_first_ref, corner_last_ref,
):
    frames, width, channels = key_ref.shape
    gain_row = gain_ref[...]
    heads = channels // LANES
    edges = ((first_ref, corner_first_ref), (last_ref, corner_last_ref))

    def one_head(g, counts):
        lanes = head_lanes(g)
        row_on, frame_on = window_ref[g, 1], window_ref[g, 0]
        counts = tuple(c + on for c, on in zip(counts, (row_on, frame_on, row_on * frame_on)))
        slots = [jnp.maximum(c - 1, 0) for c in counts]
        for kind in range(3):
            slots_ref[kind, g] = slots[kind]
        slots_ref[3, jnp.where(row_on * frame_on == 1, slots[2], heads - 1 - (g - counts[2]))] = g
        pairs = []
        for f in range(frames):
            full_rows = key_ref[f, :, lanes].astype(jnp.float32)
            pairs.append(
                ((full_rows * rms_inverse(full_rows) * gain_row).astype(jnp.bfloat16), value_ref[f, :, lanes])
            )
            for c in range(2):
                own_ref[f, c, :, lanes] = pairs[f][c]

        @pl.when(row_on == 1)
        def _():
            for f in range(frames):
                for c in range(2):
                    row_ref[slots[0], f, c] = pairs[f][c]

        @pl.when(frame_on == 1)
        def _():
            for f in range(frames):
                for c in range(2):
                    edges[f][0][slots[1], c] = pairs[f][c]

        @pl.when(row_on * frame_on == 1)
        def _():
            for f in range(frames):
                for c in range(2):
                    edges[f][1][slots[2], c] = pairs[f][c]

        return counts

    zero = jnp.int32(0)
    counts = lax.fori_loop(0, heads, one_head, (zero, zero, zero))
    slots_ref[4, 0] = counts[2]


def pack(window, key_raw, values, key_gain, sizes):
    frames, width, channels = key_raw.shape
    kinds = jax.ShapeDtypeStruct
    low = jnp.bfloat16
    shapes = [(frames, 2, width, channels), (sizes[0], frames, 2, width, LANES)]
    shapes += [(sizes[1], 2, width, LANES)] * 2 + [(sizes[2], 2, width, LANES)] * 2
    return pl.pallas_call(
        pack_kernel,
        in_specs=[whole(pltpu.SMEM)] + [whole()] * 3,
        out_specs=[whole(pltpu.SMEM)] + [whole()] * 6,
        out_shape=[kinds((5, channels // LANES), jnp.int32)] + [kinds(shape, low) for shape in shapes],
        compiler_params=params(),
        name="pack_keys_values",
    )(window, key_raw, values, key_gain)


def matmul(a, b, dims):
    return lax.dot_general(a, b, (dims, ((), ())), preferred_element_type=jnp.float32)


def attend_kernel(
    window_ref, slots_ref, query_ref, grad_ref, own_ref, chip_ref, off_ref,
    prev_ref, next_ref, chip_prev_ref, chip_next_ref, off_prev_ref, off_next_ref,
    q_gain_ref, k_gain_ref,
    query_grad_ref, own_out, chip_out, off_out, prev_out, next_out, gain_out,
    key_buf, value_buf, key_sum, value_sum, gap_ref,
):
    frames, width, _ = query_ref.shape
    heads = window_ref.shape[0]
    scale = LANES ** (-0.5)
    row_slots = chip_ref.shape[0]
    both = range(frames)
    key_buf[...] = jnp.zeros_like(key_buf)
    value_buf[...] = jnp.zeros_like(value_buf)
    gain_out[...] = jnp.zeros_like(gain_out)
    queries, keys = gap_ref.shape
    q_tile = lax.broadcasted_iota(jnp.int32, (queries, LANES), 0) // TILE_W
    for first in range(0, keys, LANES):
        k_ids = first + lax.broadcasted_iota(jnp.int32, (8, LANES), 1)
        k_tile = (k_ids % width // TILE_W)[0:1]
        gap_ref[:, first : first + LANES] = jnp.abs(q_tile - k_tile).astype(jnp.float32)
    gain_row = q_gain_ref[...]
    full, part = span_sizes(width)
    t, h = lax.axis_index("tm"), lax.axis_index("height")
    has_off = jnp.logical_and(h > 0, h < lax.axis_size("height") - 1).astype(jnp.int32)
    has_prev = (t > 0).astype(jnp.int32)
    has_next = (t < lax.axis_size("tm") - 1).astype(jnp.int32)

    def each_block(g, do):
        frame_reach, row_reach = window_ref[g, 0], window_ref[g, 1]
        row_count = 1 + 2 * row_reach
        row_slot, frame_slot, corner_slot = slots_ref[0, g], slots_ref[1, g], slots_ref[2, g]
        lanes = head_lanes(g)

        def place(r, e):
            return pl.ds(pl.multiple_of((e * row_count + r) * width, 16), width)

        for f in both:
            do(place(0, f + 1), own_ref.at[f, :, :, lanes], own_out.at[g, f])

        @pl.when(frame_reach == 1)
        def _():
            do(place(0, 0), prev_ref.at[frame_slot], prev_out.at[frame_slot])
            do(place(0, frames + 1), next_ref.at[frame_slot], next_out.at[frame_slot])

        @pl.when(row_reach == 1)
        def _():
            for f in both:
                do(place(1, f + 1), chip_ref.at[row_slot, f], chip_out.at[row_slot, f])
                do(place(2, f + 1), off_ref.at[row_slot, f], off_out.at[row_slot, f])

        @pl.when(frame_reach * row_reach == 1)
        def _():
            last = row_slots + corner_slot
            do(place(1, 0), chip_prev_ref.at[frame_slot], chip_out.at[last, 0])
            do(place(1, frames + 1), chip_next_ref.at[frame_slot], chip_out.at[last, 1])
            do(place(2, 0), off_prev_ref.at[corner_slot], off_out.at[last, 0])
            do(place(2, frames + 1), off_next_ref.at[corner_slot], off_out.at[last, 1])

    def work(group, counted, keys):
        for n, g in enumerate(group):

            def load(place, source, _, n=n):
                key_buf[n, place] = source[0]
                value_buf[n, place] = source[1]

            each_block(g, load)
        gap = gap_ref[:, 0:keys]
        k_ids = lax.broadcasted_iota(jnp.int32, (1, keys), 1)
        chains = [(n, f) for n in range(len(group)) for f in both]
        spans, inside, unit, inverse, queries, grads = {}, {}, {}, {}, {}, {}
        for n, g in enumerate(group):
            frame_reach, row_reach = window_ref[g, 0], window_ref[g, 1]
            tile_reach = window_ref[g, 2].astype(jnp.float32)
            lanes = head_lanes(g)
            per_frame = (1 + 2 * row_reach) * width
            frame = jnp.zeros_like(k_ids)
            for m in range(1, 4):
                frame += (k_ids >= m * per_frame).astype(jnp.int32)
            rest = k_ids - frame * per_frame
            off_row = jnp.logical_and(rest >= 2 * width, has_off == 0)
            for f in both:
                begin = f + 1 - frame_reach
                spans[n, f] = pl.ds(pl.multiple_of(begin * per_frame, 16), keys)
                shut = jnp.logical_or(frame > 2 * frame_reach, off_row)
                shut = jnp.logical_or(shut, jnp.logical_and(begin + frame == 0, has_prev == 0))
                shut = jnp.logical_or(shut, jnp.logical_and(begin + frame == frames + 1, has_next == 0))
                inside[n, f] = gap + jnp.where(shut, BLOCKED, 0.0) <= tile_reach
                full_rows = query_ref[f, :, lanes].astype(jnp.float32)
                inverse[n, f] = rms_inverse(full_rows)
                unit[n, f] = full_rows * inverse[n, f]
                queries[n, f] = (unit[n, f] * gain_row).astype(jnp.bfloat16)
                grads[n, f] = grad_ref[f, :, lanes]
            key_sum[n, pl.ds(pl.multiple_of((1 - frame_reach) * per_frame + keys, 16), 3 * width)] = jnp.zeros(
                (3 * width, LANES), jnp.float32
            )
            value_sum[n, pl.ds(pl.multiple_of((1 - frame_reach) * per_frame + keys, 16), 3 * width)] = jnp.zeros(
                (3 * width, LANES), jnp.float32
            )
        scores = {i: matmul(queries[i], key_buf[i[0], spans[i]], ((1,), (1,))) for i in chains}
        prob_back = {i: matmul(grads[i], value_buf[i[0], spans[i]], ((1,), (1,))) for i in chains}
        weight = {i: jnp.where(inside[i], jnp.exp2(scores[i] * (scale * LOG2E)), 0.0) for i in chains}
        over = {i: 1.0 / jnp.sum(weight[i], axis=-1, keepdims=True) for i in chains}
        delta = {i: jnp.sum(weight[i] * prob_back[i], axis=-1, keepdims=True) * over[i] for i in chains}
        prob = {i: weight[i] * over[i] for i in chains}
        score_back = {i: (prob[i] * ((prob_back[i] - delta[i]) * scale)).astype(jnp.bfloat16) for i in chains}
        query_back = {i: matmul(score_back[i], key_buf[i[0], spans[i]], ((1,), (0,))) for i in chains}
        key_back = {i: matmul(score_back[i], queries[i], ((0,), (0,))) for i in chains}
        value_back = {i: matmul(prob[i].astype(jnp.bfloat16), grads[i], ((0,), (0,))) for i in chains}
        for i in chains:
            n, f = i
            if f == 0:
                key_sum[n, spans[i]] = key_back[i]
                value_sum[n, spans[i]] = value_back[i]
            else:
                key_sum[n, spans[i]] += key_back[i]
                value_sum[n, spans[i]] += value_back[i]
            result = norm_backward(query_back[i], unit[i], inverse[i], gain_row)
            query_grad_ref[f, :, head_lanes(group[n])] = result.astype(query_grad_ref.dtype)
        first = jnp.zeros((1, LANES), jnp.float32)
        second = first
        for i in chains:
            once = counted[i[0]]
            first += once * jnp.sum(query_back[i] * unit[i], axis=0, keepdims=True)
            second += once * jnp.sum(query_back[i] * queries[i].astype(jnp.float32), axis=0, keepdims=True)
        gain_out[0:1] += first
        gain_out[1:2] += second / k_gain_ref[...]
        for n, g in enumerate(group):

            def store(place, _, out, n=n):
                out[0] = key_sum[n, place].astype(out.dtype)
                out[1] = value_sum[n, place].astype(out.dtype)

            each_block(g, store)

    wide = slots_ref[4, 0]

    def one_wide(i, carry):
        work([slots_ref[3, i]], [1.0], full)
        return carry

    def narrow_group(j, carry):
        places = [wide + GROUP * j + n for n in range(GROUP)]
        group = [slots_ref[3, jnp.minimum(place, heads - 1)] for place in places]
        work(group, [(place < heads).astype(jnp.float32) for place in places], part)
        return carry

    lax.fori_loop(0, wide, one_wide, 0)
    lax.fori_loop(0, (heads - wide + GROUP - 1) // GROUP, narrow_group, 0)


def span_sizes(width):
    return tuple(-(-blocks * width // LANES) * LANES for blocks in (9, 3))


def attend(window, slots, query_raw, out_grad, own, chip, off, edges, corners, query_gain, key_gain):
    frames, width, channels = query_raw.shape
    heads = channels // LANES
    kinds = jax.ShapeDtypeStruct
    sent_shape = (chip.shape[0] + corners[0].shape[0], frames, 2, width, LANES)
    edge_shape = edges[0].shape
    most = 3 * width + span_sizes(width)[0]
    return pl.pallas_call(
        attend_kernel,
        in_specs=[whole(pltpu.SMEM)] * 2 + [whole()] * 13,
        out_specs=[whole()] * 7,
        out_shape=[
            kinds(query_raw.shape, jnp.bfloat16),
            kinds((heads, frames, 2, width, LANES), jnp.float32),
            kinds(sent_shape, jnp.bfloat16),
            kinds(sent_shape, jnp.bfloat16),
            kinds(edge_shape, jnp.float32),
            kinds(edge_shape, jnp.float32),
            kinds((2, LANES), jnp.float32),
        ],
        scratch_shapes=[
            pltpu.VMEM((GROUP, most, LANES), jnp.bfloat16),
            pltpu.VMEM((GROUP, most, LANES), jnp.bfloat16),
            pltpu.VMEM((GROUP, most, LANES), jnp.float32),
            pltpu.VMEM((GROUP, most, LANES), jnp.float32),
            pltpu.VMEM((width, span_sizes(width)[0]), jnp.float32),
        ],
        compiler_params=params(),
        name="attend",
    )(window, slots, query_raw, out_grad, own, chip, off, *edges, *corners, query_gain, key_gain)


def relay_kernel(row_slots, window_ref, slots_ref, prev_ref, next_ref, chip_ref, off_ref, prev_out, next_out):

    def one_head(g, carry):
        row_on, frame_on = window_ref[g, 1], window_ref[g, 0]
        corner_slot, frame_slot = row_slots + slots_ref[2, g], slots_ref[1, g]

        @pl.when(jnp.logical_and(frame_on == 1, row_on == 0))
        def _():
            for kept, out in ((prev_ref, prev_out), (next_ref, next_out)):
                out[frame_slot] = kept[frame_slot].astype(out.dtype)

        @pl.when(jnp.logical_and(frame_on == 1, row_on == 1))
        def _():
            for kept, out, e in ((prev_ref, prev_out, 0), (next_ref, next_out, 1)):
                terms = kept[frame_slot] + chip_ref[corner_slot, e].astype(jnp.float32)
                out[frame_slot] = (terms + off_ref[corner_slot, e].astype(jnp.float32)).astype(out.dtype)

        return carry

    lax.fori_loop(0, window_ref.shape[0], one_head, 0)


def relay(window, slots, kept, chip, off, row_slots):
    return pl.pallas_call(
        functools.partial(relay_kernel, row_slots),
        in_specs=[whole(pltpu.SMEM)] * 2 + [whole()] * 4,
        out_specs=[whole()] * 2,
        out_shape=[jax.ShapeDtypeStruct(kept[0].shape, jnp.bfloat16)] * 2,
        compiler_params=params(),
        name="add_corner_terms",
    )(window, slots, *kept, chip, off)


def finish_kernel(
    window_ref, slots_ref, key_ref, own_ref, chip_ref, off_ref, first_ref, last_ref, gain_ref,
    key_grad_ref, value_grad_ref,
):
    frames = key_ref.shape[0]
    gain_row = gain_ref[...]
    edges = (first_ref, last_ref)

    def one_head(g, carry):
        lanes = head_lanes(g)
        row_on, frame_on = window_ref[g, 1] == 1, window_ref[g, 0] == 1
        row_slot, frame_slot = slots_ref[0, g], slots_ref[1, g]
        for f in range(frames):
            sums = []
            for c in range(2):
                rows = chip_ref[row_slot, f, c].astype(jnp.float32) + off_ref[row_slot, f, c].astype(jnp.float32)
                edge = edges[f][frame_slot, c].astype(jnp.float32)
                sums.append(own_ref[g, f, c] + jnp.where(row_on, rows, 0.0) + jnp.where(frame_on, edge, 0.0))
            full_rows = key_ref[f, :, lanes].astype(jnp.float32)
            inverse = rms_inverse(full_rows)
            result = norm_backward(sums[0], full_rows * inverse, inverse, gain_row)
            key_grad_ref[f, :, lanes] = result.astype(key_grad_ref.dtype)
            value_grad_ref[f, :, lanes] = sums[1].astype(value_grad_ref.dtype)
        return carry

    lax.fori_loop(0, window_ref.shape[0], one_head, 0, unroll=2)


def finish(window, slots, key_raw, own, chip, off, edges, key_gain):
    frames, width, _ = key_raw.shape
    return pl.pallas_call(
        finish_kernel,
        in_specs=[whole(pltpu.SMEM)] * 2 + [whole()] * 7,
        out_specs=[whole()] * 2,
        out_shape=[jax.ShapeDtypeStruct(key_raw.shape, jnp.bfloat16)] * 2,
        compiler_params=params(),
        name="finish_keys",
    )(window, slots, key_raw, own, chip, off, *edges, key_gain)


def off_chip(h):
    return h + 1 if h % 2 else h - 1


def move(block, frame_step, row_rule):
    frames_size, rows_size = lax.axis_size("tm"), lax.axis_size("height")
    route = []
    for t in range(frames_size):
        for h in range(rows_size):
            to_t, to_h = t + frame_step, row_rule(h)
            if 0 <= to_t < frames_size and 0 <= to_h < rows_size:
                route.append((t * rows_size + h, to_t * rows_size + to_h))
    return lax.ppermute(block, BOTH, route)


def same_row(h):
    return h


def chip_row(h):
    return h ^ 1


def sum_over_rows(part):
    rows_size = lax.axis_size("height")
    per_row = LANES // rows_size
    pieces = part.reshape(2, rows_size, per_row).transpose(1, 0, 2).reshape(rows_size, 2 * per_row)
    return lax.all_to_all(pieces, "height", 0, 0, tiled=True).sum(0, keepdims=True)


def sum_over_frames(mine):
    copies = jnp.broadcast_to(mine, (lax.axis_size("tm"), mine.shape[1]))
    return lax.all_to_all(copies, "tm", 0, 0, tiled=True).sum(0).reshape(2, mine.shape[1] // 2)


def with_sizes(sizes, query_flat, key_flat, value_flat, grad_flat, q_gain, k_gain, window):
    slots, own, rows, first, last, corner_first, corner_last = pack(window, key_flat, value_flat, k_gain, sizes)
    off = move(rows, 0, off_chip)
    prev = move(last, 1, same_row)
    following = move(first, -1, same_row)
    off_prev = move(corner_last, 1, off_chip)
    off_next = move(corner_first, -1, off_chip)
    rows, prev, following, off_prev, off_next = lax.optimization_barrier((rows, prev, following, off_prev, off_next))
    chip = move(rows, 0, chip_row)
    chip_prev = move(prev, 0, chip_row)
    chip_next = move(following, 0, chip_row)

    query_grad, own_sum, chip_sum, off_sum, prev_sum, next_sum, gain_part = attend(
        window, slots, query_flat, grad_flat, own, chip, off,
        (prev, following, chip_prev, chip_next), (off_prev, off_next), q_gain, k_gain,
    )

    off_back = move(off_sum, 0, off_chip)
    chip_back = move(chip_sum, 0, chip_row)
    mine = sum_over_rows(gain_part)
    chip_back, off_back, mine = lax.optimization_barrier((chip_back, off_back, mine))
    prev_all, next_all = relay(window, slots, (prev_sum, next_sum), chip_back, off_back, sizes[0])
    last_back = move(prev_all, -1, same_row)
    first_back = move(next_all, 1, same_row)
    gain_grad = sum_over_frames(mine)
    first_back, last_back, gain_grad = lax.optimization_barrier((first_back, last_back, gain_grad))
    key_grad, value_grad = finish(
        window, slots, key_flat, own_sum, chip_back, off_back, (first_back, last_back), k_gain
    )
    return query_grad, key_grad, value_grad, gain_grad


def on_device(query_raw, key_raw, values, out_grad, query_gain, key_gain, window):
    frames, _, width, channels = query_raw.shape
    heads = channels // LANES
    flat = (frames, width, channels)
    row_on, frame_on = window[:, 1], window[:, 0]
    row_count, frame_count, both_count = jnp.sum(row_on), jnp.sum(frame_on), jnp.sum(row_on * frame_on)
    choices = SIZES + [(heads, heads, heads)]
    choice = jnp.int32(0)
    for sizes in SIZES:
        fits = (row_count <= sizes[0]) & (frame_count <= sizes[1]) & (both_count <= sizes[2])
        choice += 1 - fits.astype(jnp.int32)
    args = [x.reshape(flat) for x in (query_raw, key_raw, values, out_grad)]
    outs = lax.switch(
        choice,
        [functools.partial(with_sizes, sizes) for sizes in choices],
        *args, query_gain[None], key_gain[None], window,
    )
    return tuple(x.reshape(query_raw.shape) for x in outs[:3]) + (outs[3],)


def solution(mesh):
    token = P("tm", "height", None, None)
    return jax.shard_map(
        on_device,
        mesh=mesh,
        in_specs=(token, token, token, token, P(), P(), P()),
        out_specs=(token, token, token, P(None, "height")),
        check_vma=False,
    )
```

```python
import functools

import jax
import jax.numpy as jnp
from jax import lax
from jax.experimental import pallas as pl
from jax.experimental.pallas import tpu as pltpu
from jax.sharding import PartitionSpec as P

TILE_W = 8
EPSILON = 1e-06
HEAD_DIM = 128
LOG2E = 1.4426950408889634
BLOCKED = 1000.0
LANES = 128
BOTH = ("tm", "height")
SIZES = [(6, 6, 4), (8, 8, 6), (10, 10, 8)]
GROUP = 3
VMEM_BYTES = 56 * 1024 * 1024


def rms_inverse(full_rows):
    return lax.rsqrt(jnp.mean(full_rows * full_rows, axis=-1, keepdims=True) + EPSILON)


def norm_backward(grad_rows, unit_rows, inverse, gain_row):
    scaled = grad_rows * gain_row
    return inverse * (scaled - unit_rows * jnp.mean(unit_rows * scaled, axis=-1, keepdims=True))


def whole(memory_space=pltpu.VMEM):
    return pl.BlockSpec(memory_space=memory_space)


def params():
    return pltpu.CompilerParams(vmem_limit_bytes=VMEM_BYTES)


def head_lanes(g):
    return pl.ds(pl.multiple_of(g * LANES, LANES), LANES)


def pack_kernel(
    window_ref, key_ref, value_ref, gain_ref,
    slots_ref, own_ref, row_ref, first_ref, last_ref, corner_first_ref, corner_last_ref,
):
    frames, width, channels = key_ref.shape
    gain_row = gain_ref[...]
    heads = channels // LANES
    edges = ((first_ref, corner_first_ref), (last_ref, corner_last_ref))

    def one_head(g, counts):
        lanes = head_lanes(g)
        row_on, frame_on = window_ref[g, 1], window_ref[g, 0]
        counts = tuple(c + on for c, on in zip(counts, (row_on, frame_on, row_on * frame_on)))
        slots = [jnp.maximum(c - 1, 0) for c in counts]
        for kind in range(3):
            slots_ref[kind, g] = slots[kind]
        slots_ref[3, jnp.where(row_on * frame_on == 1, slots[2], heads - 1 - (g - counts[2]))] = g
        pairs = []
        for f in range(frames):
            full_rows = key_ref[f, :, lanes].astype(jnp.float32)
            pairs.append(
                ((full_rows * rms_inverse(full_rows) * gain_row).astype(jnp.bfloat16), value_ref[f, :, lanes])
            )
            for c in range(2):
                own_ref[f, c, :, lanes] = pairs[f][c]

        @pl.when(row_on == 1)
        def _():
            for f in range(frames):
                for c in range(2):
                    row_ref[slots[0], f, c] = pairs[f][c]

        @pl.when(frame_on == 1)
        def _():
            for f in range(frames):
                for c in range(2):
                    edges[f][0][slots[1], c] = pairs[f][c]

        @pl.when(row_on * frame_on == 1)
        def _():
            for f in range(frames):
                for c in range(2):
                    edges[f][1][slots[2], c] = pairs[f][c]

        return counts

    zero = jnp.int32(0)
    counts = lax.fori_loop(0, heads, one_head, (zero, zero, zero))
    slots_ref[4, 0] = counts[2]


def pack(window, key_raw, values, key_gain, sizes):
    frames, width, channels = key_raw.shape
    kinds = jax.ShapeDtypeStruct
    low = jnp.bfloat16
    shapes = [(frames, 2, width, channels), (sizes[0], frames, 2, width, LANES)]
    shapes += [(sizes[1], 2, width, LANES)] * 2 + [(sizes[2], 2, width, LANES)] * 2
    return pl.pallas_call(
        pack_kernel,
        in_specs=[whole(pltpu.SMEM)] + [whole()] * 3,
        out_specs=[whole(pltpu.SMEM)] + [whole()] * 6,
        out_shape=[kinds((5, channels // LANES), jnp.int32)] + [kinds(shape, low) for shape in shapes],
        compiler_params=params(),
        name="pack_keys_values",
    )(window, key_raw, values, key_gain)


def matmul(a, b, dims):
    return lax.dot_general(a, b, (dims, ((), ())), preferred_element_type=jnp.float32)


def attend_kernel(
    window_ref, slots_ref, query_ref, grad_ref, own_ref, chip_ref, off_ref,
    prev_ref, next_ref, chip_prev_ref, chip_next_ref, off_prev_ref, off_next_ref,
    q_gain_ref, k_gain_ref,
    query_grad_ref, own_out, chip_out, off_out, prev_out, next_out, gain_out,
    key_buf, value_buf, key_sum, value_sum, gap_ref,
):
    frames, width, _ = query_ref.shape
    heads = window_ref.shape[0]
    scale = LANES ** (-0.5)
    row_slots = chip_ref.shape[0]
    both = range(frames)
    key_buf[...] = jnp.zeros_like(key_buf)
    value_buf[...] = jnp.zeros_like(value_buf)
    gain_out[...] = jnp.zeros_like(gain_out)
    queries, keys = gap_ref.shape
    q_tile = lax.broadcasted_iota(jnp.int32, (queries, LANES), 0) // TILE_W
    for first in range(0, keys, LANES):
        k_ids = first + lax.broadcasted_iota(jnp.int32, (8, LANES), 1)
        k_tile = (k_ids % width // TILE_W)[0:1]
        gap_ref[:, first : first + LANES] = jnp.abs(q_tile - k_tile).astype(jnp.float32)
    gain_row = q_gain_ref[...]
    full, part = span_sizes(width)
    t, h = lax.axis_index("tm"), lax.axis_index("height")
    has_off = jnp.logical_and(h > 0, h < lax.axis_size("height") - 1).astype(jnp.int32)
    has_prev = (t > 0).astype(jnp.int32)
    has_next = (t < lax.axis_size("tm") - 1).astype(jnp.int32)

    def each_block(g, do):
        frame_reach, row_reach = window_ref[g, 0], window_ref[g, 1]
        row_count = 1 + 2 * row_reach
        row_slot, frame_slot, corner_slot = slots_ref[0, g], slots_ref[1, g], slots_ref[2, g]
        lanes = head_lanes(g)

        def place(r, e):
            return pl.ds(pl.multiple_of((e * row_count + r) * width, 16), width)

        for f in both:
            do(place(0, f + 1), own_ref.at[f, :, :, lanes], own_out.at[g, f])

        @pl.when(frame_reach == 1)
        def _():
            do(place(0, 0), prev_ref.at[frame_slot], prev_out.at[frame_slot])
            do(place(0, frames + 1), next_ref.at[frame_slot], next_out.at[frame_slot])

        @pl.when(row_reach == 1)
        def _():
            for f in both:
                do(place(1, f + 1), chip_ref.at[row_slot, f], chip_out.at[row_slot, f])
                do(place(2, f + 1), off_ref.at[row_slot, f], off_out.at[row_slot, f])

        @pl.when(frame_reach * row_reach == 1)
        def _():
            last = row_slots + corner_slot
            do(place(1, 0), chip_prev_ref.at[frame_slot], chip_out.at[last, 0])
            do(place(1, frames + 1), chip_next_ref.at[frame_slot], chip_out.at[last, 1])
            do(place(2, 0), off_prev_ref.at[corner_slot], off_out.at[last, 0])
            do(place(2, frames + 1), off_next_ref.at[corner_slot], off_out.at[last, 1])

    def work(group, counted, keys):
        for n, g in enumerate(group):

            def load(place, source, _, n=n):
                key_buf[n, place] = source[0]
                value_buf[n, place] = source[1]

            each_block(g, load)
        gap = gap_ref[:, 0:keys]
        k_ids = lax.broadcasted_iota(jnp.int32, (1, keys), 1)
        chains = [(n, f) for n in range(len(group)) for f in both]
        spans, inside, unit, inverse, queries, grads = {}, {}, {}, {}, {}, {}
        for n, g in enumerate(group):
            frame_reach, row_reach = window_ref[g, 0], window_ref[g, 1]
            tile_reach = window_ref[g, 2].astype(jnp.float32)
            lanes = head_lanes(g)
            per_frame = (1 + 2 * row_reach) * width
            frame = jnp.zeros_like(k_ids)
            for m in range(1, 4):
                frame += (k_ids >= m * per_frame).astype(jnp.int32)
            rest = k_ids - frame * per_frame
            off_row = jnp.logical_and(rest >= 2 * width, has_off == 0)
            for f in both:
                begin = f + 1 - frame_reach
                spans[n, f] = pl.ds(pl.multiple_of(begin * per_frame, 16), keys)
                shut = jnp.logical_or(frame > 2 * frame_reach, off_row)
                shut = jnp.logical_or(shut, jnp.logical_and(begin + frame == 0, has_prev == 0))
                shut = jnp.logical_or(shut, jnp.logical_and(begin + frame == frames + 1, has_next == 0))
                inside[n, f] = gap + jnp.where(shut, BLOCKED, 0.0) <= tile_reach
                full_rows = query_ref[f, :, lanes].astype(jnp.float32)
                inverse[n, f] = rms_inverse(full_rows)
                unit[n, f] = full_rows * inverse[n, f]
                queries[n, f] = (unit[n, f] * gain_row).astype(jnp.bfloat16)
                grads[n, f] = grad_ref[f, :, lanes]
            key_sum[n, pl.ds(pl.multiple_of((1 - frame_reach) * per_frame + keys, 16), 3 * width)] = jnp.zeros(
                (3 * width, LANES), jnp.float32
            )
            value_sum[n, pl.ds(pl.multiple_of((1 - frame_reach) * per_frame + keys, 16), 3 * width)] = jnp.zeros(
                (3 * width, LANES), jnp.float32
            )
        scores = {i: matmul(queries[i], key_buf[i[0], spans[i]], ((1,), (1,))) for i in chains}
        prob_back = {i: matmul(grads[i], value_buf[i[0], spans[i]], ((1,), (1,))) for i in chains}
        weight = {i: jnp.where(inside[i], jnp.exp2(scores[i] * (scale * LOG2E)), 0.0) for i in chains}
        over = {i: 1.0 / jnp.sum(weight[i], axis=-1, keepdims=True) for i in chains}
        delta = {i: jnp.sum(weight[i] * prob_back[i], axis=-1, keepdims=True) * over[i] for i in chains}
        prob = {i: weight[i] * over[i] for i in chains}
        score_back = {i: (prob[i] * ((prob_back[i] - delta[i]) * scale)).astype(jnp.bfloat16) for i in chains}
        query_back = {i: matmul(score_back[i], key_buf[i[0], spans[i]], ((1,), (0,))) for i in chains}
        key_back = {i: matmul(score_back[i], queries[i], ((0,), (0,))) for i in chains}
        value_back = {i: matmul(prob[i].astype(jnp.bfloat16), grads[i], ((0,), (0,))) for i in chains}
        for i in chains:
            n, f = i
            if f == 0:
                key_sum[n, spans[i]] = key_back[i]
                value_sum[n, spans[i]] = value_back[i]
            else:
                key_sum[n, spans[i]] += key_back[i]
                value_sum[n, spans[i]] += value_back[i]
            result = norm_backward(query_back[i], unit[i], inverse[i], gain_row)
            query_grad_ref[f, :, head_lanes(group[n])] = result.astype(query_grad_ref.dtype)
        first = jnp.zeros((1, LANES), jnp.float32)
        second = first
        for i in chains:
            once = counted[i[0]]
            first += once * jnp.sum(query_back[i] * unit[i], axis=0, keepdims=True)
            second += once * jnp.sum(query_back[i] * queries[i].astype(jnp.float32), axis=0, keepdims=True)
        gain_out[0:1] += first
        gain_out[1:2] += second / k_gain_ref[...]
        for n, g in enumerate(group):

            def store(place, _, out, n=n):
                out[0] = key_sum[n, place].astype(out.dtype)
                out[1] = value_sum[n, place].astype(out.dtype)

            each_block(g, store)

    wide = slots_ref[4, 0]

    def one_wide(i, carry):
        work([slots_ref[3, i]], [1.0], full)
        return carry

    def narrow_group(j, carry):
        places = [wide + GROUP * j + n for n in range(GROUP)]
        group = [slots_ref[3, jnp.minimum(place, heads - 1)] for place in places]
        work(group, [(place < heads).astype(jnp.float32) for place in places], part)
        return carry

    lax.fori_loop(0, wide, one_wide, 0)
    lax.fori_loop(0, (heads - wide + GROUP - 1) // GROUP, narrow_group, 0)


def span_sizes(width):
    return tuple(-(-blocks * width // LANES) * LANES for blocks in (9, 3))


def attend(window, slots, query_raw, out_grad, own, chip, off, edges, corners, query_gain, key_gain):
    frames, width, channels = query_raw.shape
    heads = channels // LANES
    kinds = jax.ShapeDtypeStruct
    sent_shape = (chip.shape[0] + corners[0].shape[0], frames, 2, width, LANES)
    edge_shape = edges[0].shape
    most = 3 * width + span_sizes(width)[0]
    return pl.pallas_call(
        attend_kernel,
        in_specs=[whole(pltpu.SMEM)] * 2 + [whole()] * 13,
        out_specs=[whole()] * 7,
        out_shape=[
            kinds(query_raw.shape, jnp.bfloat16),
            kinds((heads, frames, 2, width, LANES), jnp.float32),
            kinds(sent_shape, jnp.bfloat16),
            kinds(sent_shape, jnp.bfloat16),
            kinds(edge_shape, jnp.float32),
            kinds(edge_shape, jnp.float32),
            kinds((2, LANES), jnp.float32),
        ],
        scratch_shapes=[
            pltpu.VMEM((GROUP, most, LANES), jnp.bfloat16),
            pltpu.VMEM((GROUP, most, LANES), jnp.bfloat16),
            pltpu.VMEM((GROUP, most, LANES), jnp.float32),
            pltpu.VMEM((GROUP, most, LANES), jnp.float32),
            pltpu.VMEM((width, span_sizes(width)[0]), jnp.float32),
        ],
        compiler_params=params(),
        name="attend",
    )(window, slots, query_raw, out_grad, own, chip, off, *edges, *corners, query_gain, key_gain)


def relay_kernel(row_slots, window_ref, slots_ref, prev_ref, next_ref, chip_ref, off_ref, prev_out, next_out):

    def one_head(g, carry):
        row_on, frame_on = window_ref[g, 1], window_ref[g, 0]
        corner_slot, frame_slot = row_slots + slots_ref[2, g], slots_ref[1, g]

        @pl.when(jnp.logical_and(frame_on == 1, row_on == 0))
        def _():
            for kept, out in ((prev_ref, prev_out), (next_ref, next_out)):
                out[frame_slot] = kept[frame_slot].astype(out.dtype)

        @pl.when(jnp.logical_and(frame_on == 1, row_on == 1))
        def _():
            for kept, out, e in ((prev_ref, prev_out, 0), (next_ref, next_out, 1)):
                terms = kept[frame_slot] + chip_ref[corner_slot, e].astype(jnp.float32)
                out[frame_slot] = (terms + off_ref[corner_slot, e].astype(jnp.float32)).astype(out.dtype)

        return carry

    lax.fori_loop(0, window_ref.shape[0], one_head, 0)


def relay(window, slots, kept, chip, off, row_slots):
    return pl.pallas_call(
        functools.partial(relay_kernel, row_slots),
        in_specs=[whole(pltpu.SMEM)] * 2 + [whole()] * 4,
        out_specs=[whole()] * 2,
        out_shape=[jax.ShapeDtypeStruct(kept[0].shape, jnp.bfloat16)] * 2,
        compiler_params=params(),
        name="add_corner_terms",
    )(window, slots, *kept, chip, off)


def finish_kernel(
    window_ref, slots_ref, key_ref, own_ref, chip_ref, off_ref, first_ref, last_ref, gain_ref,
    key_grad_ref, value_grad_ref,
):
    frames = key_ref.shape[0]
    gain_row = gain_ref[...]
    edges = (first_ref, last_ref)

    def one_head(g, carry):
        lanes = head_lanes(g)
        row_on, frame_on = window_ref[g, 1] == 1, window_ref[g, 0] == 1
        row_slot, frame_slot = slots_ref[0, g], slots_ref[1, g]
        for f in range(frames):
            sums = []
            for c in range(2):
                rows = chip_ref[row_slot, f, c].astype(jnp.float32) + off_ref[row_slot, f, c].astype(jnp.float32)
                edge = edges[f][frame_slot, c].astype(jnp.float32)
                sums.append(own_ref[g, f, c] + jnp.where(row_on, rows, 0.0) + jnp.where(frame_on, edge, 0.0))
            full_rows = key_ref[f, :, lanes].astype(jnp.float32)
            inverse = rms_inverse(full_rows)
            result = norm_backward(sums[0], full_rows * inverse, inverse, gain_row)
            key_grad_ref[f, :, lanes] = result.astype(key_grad_ref.dtype)
            value_grad_ref[f, :, lanes] = sums[1].astype(value_grad_ref.dtype)
        return carry

    lax.fori_loop(0, window_ref.shape[0], one_head, 0, unroll=4)


def finish(window, slots, key_raw, own, chip, off, edges, key_gain):
    frames, width, _ = key_raw.shape
    return pl.pallas_call(
        finish_kernel,
        in_specs=[whole(pltpu.SMEM)] * 2 + [whole()] * 7,
        out_specs=[whole()] * 2,
        out_shape=[jax.ShapeDtypeStruct(key_raw.shape, jnp.bfloat16)] * 2,
        compiler_params=params(),
        name="finish_keys",
    )(window, slots, key_raw, own, chip, off, *edges, key_gain)


def off_chip(h):
    return h + 1 if h % 2 else h - 1


def move(block, frame_step, row_rule):
    frames_size, rows_size = lax.axis_size("tm"), lax.axis_size("height")
    route = []
    for t in range(frames_size):
        for h in range(rows_size):
            to_t, to_h = t + frame_step, row_rule(h)
            if 0 <= to_t < frames_size and 0 <= to_h < rows_size:
                route.append((t * rows_size + h, to_t * rows_size + to_h))
    return lax.ppermute(block, BOTH, route)


def same_row(h):
    return h


def chip_row(h):
    return h ^ 1


def sum_over_rows(part):
    rows_size = lax.axis_size("height")
    per_row = LANES // rows_size
    pieces = part.reshape(2, rows_size, per_row).transpose(1, 0, 2).reshape(rows_size, 2 * per_row)
    return lax.all_to_all(pieces, "height", 0, 0, tiled=True).sum(0, keepdims=True)


def sum_over_frames(mine):
    copies = jnp.broadcast_to(mine, (lax.axis_size("tm"), mine.shape[1]))
    return lax.all_to_all(copies, "tm", 0, 0, tiled=True).sum(0).reshape(2, mine.shape[1] // 2)


def with_sizes(sizes, query_flat, key_flat, value_flat, grad_flat, q_gain, k_gain, window):
    slots, own, rows, first, last, corner_first, corner_last = pack(window, key_flat, value_flat, k_gain, sizes)
    off = move(rows, 0, off_chip)
    prev = move(last, 1, same_row)
    following = move(first, -1, same_row)
    off_prev = move(corner_last, 1, off_chip)
    off_next = move(corner_first, -1, off_chip)
    rows, off_prev, off_next = lax.optimization_barrier((rows, off_prev, off_next))
    chip = move(rows, 0, chip_row)
    chip_prev = move(prev, 0, chip_row)
    chip_next = move(following, 0, chip_row)

    query_grad, own_sum, chip_sum, off_sum, prev_sum, next_sum, gain_part = attend(
        window, slots, query_flat, grad_flat, own, chip, off,
        (prev, following, chip_prev, chip_next), (off_prev, off_next), q_gain, k_gain,
    )

    off_back = move(off_sum, 0, off_chip)
    chip_back = move(chip_sum, 0, chip_row)
    mine = sum_over_rows(gain_part)
    chip_back, off_back, mine = lax.optimization_barrier((chip_back, off_back, mine))
    prev_all, next_all = relay(window, slots, (prev_sum, next_sum), chip_back, off_back, sizes[0])
    last_back = move(prev_all, -1, same_row)
    first_back = move(next_all, 1, same_row)
    gain_grad = sum_over_frames(mine)
    first_back, last_back, gain_grad = lax.optimization_barrier((first_back, last_back, gain_grad))
    key_grad, value_grad = finish(
        window, slots, key_flat, own_sum, chip_back, off_back, (first_back, last_back), k_gain
    )
    return query_grad, key_grad, value_grad, gain_grad


def on_device(query_raw, key_raw, values, out_grad, query_gain, key_gain, window):
    frames, _, width, channels = query_raw.shape
    heads = channels // LANES
    flat = (frames, width, channels)
    row_on, frame_on = window[:, 1], window[:, 0]
    row_count, frame_count, both_count = jnp.sum(row_on), jnp.sum(frame_on), jnp.sum(row_on * frame_on)
    choices = SIZES + [(heads, heads, heads)]
    choice = jnp.int32(0)
    for sizes in SIZES:
        fits = (row_count <= sizes[0]) & (frame_count <= sizes[1]) & (both_count <= sizes[2])
        choice += 1 - fits.astype(jnp.int32)
    args = [x.reshape(flat) for x in (query_raw, key_raw, values, out_grad)]
    outs = lax.switch(
        choice,
        [functools.partial(with_sizes, sizes) for sizes in choices],
        *args, query_gain[None], key_gain[None], window,
    )
    return tuple(x.reshape(query_raw.shape) for x in outs[:3]) + (outs[3],)


def solution(mesh):
    token = P("tm", "height", None, None)
    return jax.shard_map(
        on_device,
        mesh=mesh,
        in_specs=(token, token, token, token, P(), P(), P()),
        out_specs=(token, token, token, P(None, "height")),
        check_vma=False,
    )
```

```python
import functools

import jax
import jax.numpy as jnp
from jax import lax
from jax.experimental import pallas as pl
from jax.experimental.pallas import tpu as pltpu
from jax.sharding import PartitionSpec as P

TILE_W = 8
EPSILON = 1e-06
HEAD_DIM = 128
LOG2E = 1.4426950408889634
BLOCKED = 1000.0
LANES = 128
BOTH = ("tm", "height")
SIZES = [(6, 6, 4), (8, 8, 6), (10, 10, 8)]
GROUP = 3
VMEM_BYTES = 56 * 1024 * 1024


def rms_inverse(full_rows):
    return lax.rsqrt(jnp.mean(full_rows * full_rows, axis=-1, keepdims=True) + EPSILON)


def norm_backward(grad_rows, unit_rows, inverse, gain_row):
    scaled = grad_rows * gain_row
    return inverse * (scaled - unit_rows * jnp.mean(unit_rows * scaled, axis=-1, keepdims=True))


def whole(memory_space=pltpu.VMEM):
    return pl.BlockSpec(memory_space=memory_space)


def params():
    return pltpu.CompilerParams(vmem_limit_bytes=VMEM_BYTES)


def head_lanes(g):
    return pl.ds(pl.multiple_of(g * LANES, LANES), LANES)


def pack_kernel(
    window_ref, key_ref, value_ref, gain_ref,
    slots_ref, own_ref, row_ref, first_ref, last_ref, corner_first_ref, corner_last_ref,
):
    frames, width, channels = key_ref.shape
    gain_row = gain_ref[...]
    heads = channels // LANES
    edges = ((first_ref, corner_first_ref), (last_ref, corner_last_ref))

    def one_norm(g, carry):
        lanes = head_lanes(g)
        for f in range(frames):
            full_rows = key_ref[f, :, lanes].astype(jnp.float32)
            own_ref[f, 0, :, lanes] = (full_rows * rms_inverse(full_rows) * gain_row).astype(jnp.bfloat16)
            own_ref[f, 1, :, lanes] = value_ref[f, :, lanes]
        return carry

    lax.fori_loop(0, heads, one_norm, 0, unroll=4)

    def one_head(g, counts):
        lanes = head_lanes(g)
        row_on, frame_on = window_ref[g, 1], window_ref[g, 0]
        counts = tuple(c + on for c, on in zip(counts, (row_on, frame_on, row_on * frame_on)))
        slots = [jnp.maximum(c - 1, 0) for c in counts]
        for kind in range(3):
            slots_ref[kind, g] = slots[kind]
        slots_ref[3, jnp.where(row_on * frame_on == 1, slots[2], heads - 1 - (g - counts[2]))] = g

        @pl.when(row_on == 1)
        def _():
            row_ref[slots[0]] = own_ref[:, :, :, lanes]

        @pl.when(frame_on == 1)
        def _():
            for f in range(frames):
                edges[f][0][slots[1]] = own_ref[f, :, :, lanes]

        @pl.when(row_on * frame_on == 1)
        def _():
            for f in range(frames):
                edges[f][1][slots[2]] = own_ref[f, :, :, lanes]

        return counts

    zero = jnp.int32(0)
    counts = lax.fori_loop(0, heads, one_head, (zero, zero, zero))
    slots_ref[4, 0] = counts[2]


def pack(window, key_raw, values, key_gain, sizes):
    frames, width, channels = key_raw.shape
    kinds = jax.ShapeDtypeStruct
    low = jnp.bfloat16
    shapes = [(frames, 2, width, channels), (sizes[0], frames, 2, width, LANES)]
    shapes += [(sizes[1], 2, width, LANES)] * 2 + [(sizes[2], 2, width, LANES)] * 2
    return pl.pallas_call(
        pack_kernel,
        in_specs=[whole(pltpu.SMEM)] + [whole()] * 3,
        out_specs=[whole(pltpu.SMEM)] + [whole()] * 6,
        out_shape=[kinds((5, channels // LANES), jnp.int32)] + [kinds(shape, low) for shape in shapes],
        compiler_params=params(),
        name="pack_keys_values",
    )(window, key_raw, values, key_gain)


def matmul(a, b, dims):
    return lax.dot_general(a, b, (dims, ((), ())), preferred_element_type=jnp.float32)


def attend_kernel(
    window_ref, slots_ref, query_ref, grad_ref, own_ref, chip_ref, off_ref,
    prev_ref, next_ref, chip_prev_ref, chip_next_ref, off_prev_ref, off_next_ref,
    q_gain_ref, k_gain_ref,
    query_grad_ref, own_out, chip_out, off_out, prev_out, next_out, gain_out,
    key_buf, value_buf, key_sum, value_sum, gap_ref,
):
    frames, width, _ = query_ref.shape
    heads = window_ref.shape[0]
    scale = LANES ** (-0.5)
    row_slots = chip_ref.shape[0]
    both = range(frames)
    key_buf[...] = jnp.zeros_like(key_buf)
    value_buf[...] = jnp.zeros_like(value_buf)
    gain_out[...] = jnp.zeros_like(gain_out)
    queries, keys = gap_ref.shape
    q_tile = lax.broadcasted_iota(jnp.int32, (queries, LANES), 0) // TILE_W
    for first in range(0, keys, LANES):
        k_ids = first + lax.broadcasted_iota(jnp.int32, (8, LANES), 1)
        k_tile = (k_ids % width // TILE_W)[0:1]
        gap_ref[:, first : first + LANES] = jnp.abs(q_tile - k_tile).astype(jnp.float32)
    gain_row = q_gain_ref[...]
    full, part = span_sizes(width)
    t, h = lax.axis_index("tm"), lax.axis_index("height")
    has_off = jnp.logical_and(h > 0, h < lax.axis_size("height") - 1).astype(jnp.int32)
    has_prev = (t > 0).astype(jnp.int32)
    has_next = (t < lax.axis_size("tm") - 1).astype(jnp.int32)

    def each_block(g, do):
        frame_reach, row_reach = window_ref[g, 0], window_ref[g, 1]
        row_count = 1 + 2 * row_reach
        row_slot, frame_slot, corner_slot = slots_ref[0, g], slots_ref[1, g], slots_ref[2, g]
        lanes = head_lanes(g)

        def place(r, e):
            return pl.ds(pl.multiple_of((e * row_count + r) * width, 16), width)

        for f in both:
            do(place(0, f + 1), own_ref.at[f, :, :, lanes], own_out.at[g, f])

        @pl.when(frame_reach == 1)
        def _():
            do(place(0, 0), prev_ref.at[frame_slot], prev_out.at[frame_slot])
            do(place(0, frames + 1), next_ref.at[frame_slot], next_out.at[frame_slot])

        @pl.when(row_reach == 1)
        def _():
            for f in both:
                do(place(1, f + 1), chip_ref.at[row_slot, f], chip_out.at[row_slot, f])
                do(place(2, f + 1), off_ref.at[row_slot, f], off_out.at[row_slot, f])

        @pl.when(frame_reach * row_reach == 1)
        def _():
            last = row_slots + corner_slot
            do(place(1, 0), chip_prev_ref.at[frame_slot], chip_out.at[last, 0])
            do(place(1, frames + 1), chip_next_ref.at[frame_slot], chip_out.at[last, 1])
            do(place(2, 0), off_prev_ref.at[corner_slot], off_out.at[last, 0])
            do(place(2, frames + 1), off_next_ref.at[corner_slot], off_out.at[last, 1])

    def work(group, counted, keys):
        for n, g in enumerate(group):

            def load(place, source, _, n=n):
                key_buf[n, place] = source[0]
                value_buf[n, place] = source[1]

            each_block(g, load)
        gap = gap_ref[:, 0:keys]
        k_ids = lax.broadcasted_iota(jnp.int32, (1, keys), 1)
        chains = [(n, f) for n in range(len(group)) for f in both]
        spans, inside, unit, inverse, queries, grads = {}, {}, {}, {}, {}, {}
        for n, g in enumerate(group):
            frame_reach, row_reach = window_ref[g, 0], window_ref[g, 1]
            tile_reach = window_ref[g, 2].astype(jnp.float32)
            lanes = head_lanes(g)
            per_frame = (1 + 2 * row_reach) * width
            frame = jnp.zeros_like(k_ids)
            for m in range(1, 4):
                frame += (k_ids >= m * per_frame).astype(jnp.int32)
            rest = k_ids - frame * per_frame
            off_row = jnp.logical_and(rest >= 2 * width, has_off == 0)
            for f in both:
                begin = f + 1 - frame_reach
                spans[n, f] = pl.ds(pl.multiple_of(begin * per_frame, 16), keys)
                shut = jnp.logical_or(frame > 2 * frame_reach, off_row)
                shut = jnp.logical_or(shut, jnp.logical_and(begin + frame == 0, has_prev == 0))
                shut = jnp.logical_or(shut, jnp.logical_and(begin + frame == frames + 1, has_next == 0))
                inside[n, f] = gap + jnp.where(shut, BLOCKED, 0.0) <= tile_reach
                full_rows = query_ref[f, :, lanes].astype(jnp.float32)
                inverse[n, f] = rms_inverse(full_rows)
                unit[n, f] = full_rows * inverse[n, f]
                queries[n, f] = (unit[n, f] * gain_row).astype(jnp.bfloat16)
                grads[n, f] = grad_ref[f, :, lanes]
            key_sum[n, pl.ds(pl.multiple_of((1 - frame_reach) * per_frame + keys, 16), 3 * width)] = jnp.zeros(
                (3 * width, LANES), jnp.float32
            )
            value_sum[n, pl.ds(pl.multiple_of((1 - frame_reach) * per_frame + keys, 16), 3 * width)] = jnp.zeros(
                (3 * width, LANES), jnp.float32
            )
        scores = {i: matmul(queries[i], key_buf[i[0], spans[i]], ((1,), (1,))) for i in chains}
        prob_back = {i: matmul(grads[i], value_buf[i[0], spans[i]], ((1,), (1,))) for i in chains}
        weight = {i: jnp.where(inside[i], jnp.exp2(scores[i] * (scale * LOG2E)), 0.0) for i in chains}
        over = {i: 1.0 / jnp.sum(weight[i], axis=-1, keepdims=True) for i in chains}
        delta = {i: jnp.sum(weight[i] * prob_back[i], axis=-1, keepdims=True) * over[i] for i in chains}
        prob = {i: weight[i] * over[i] for i in chains}
        score_back = {i: (prob[i] * ((prob_back[i] - delta[i]) * scale)).astype(jnp.bfloat16) for i in chains}
        query_back = {i: matmul(score_back[i], key_buf[i[0], spans[i]], ((1,), (0,))) for i in chains}
        key_back = {i: matmul(score_back[i], queries[i], ((0,), (0,))) for i in chains}
        value_back = {i: matmul(prob[i].astype(jnp.bfloat16), grads[i], ((0,), (0,))) for i in chains}
        for i in chains:
            n, f = i
            if f == 0:
                key_sum[n, spans[i]] = key_back[i]
                value_sum[n, spans[i]] = value_back[i]
            else:
                key_sum[n, spans[i]] += key_back[i]
                value_sum[n, spans[i]] += value_back[i]
            result = norm_backward(query_back[i], unit[i], inverse[i], gain_row)
            query_grad_ref[f, :, head_lanes(group[n])] = result.astype(query_grad_ref.dtype)
        first = jnp.zeros((1, LANES), jnp.float32)
        second = first
        for i in chains:
            once = counted[i[0]]
            first += once * jnp.sum(query_back[i] * unit[i], axis=0, keepdims=True)
            second += once * jnp.sum(query_back[i] * queries[i].astype(jnp.float32), axis=0, keepdims=True)
        gain_out[0:1] += first
        gain_out[1:2] += second / k_gain_ref[...]
        for n, g in enumerate(group):

            def store(place, _, out, n=n):
                out[0] = key_sum[n, place].astype(out.dtype)
                out[1] = value_sum[n, place].astype(out.dtype)

            each_block(g, store)

    wide = slots_ref[4, 0]

    def one_wide(i, carry):
        work([slots_ref[3, i]], [1.0], full)
        return carry

    def narrow_group(j, carry):
        places = [wide + GROUP * j + n for n in range(GROUP)]
        group = [slots_ref[3, jnp.minimum(place, heads - 1)] for place in places]
        work(group, [(place < heads).astype(jnp.float32) for place in places], part)
        return carry

    lax.fori_loop(0, wide, one_wide, 0)
    lax.fori_loop(0, (heads - wide + GROUP - 1) // GROUP, narrow_group, 0)


def span_sizes(width):
    return tuple(-(-blocks * width // LANES) * LANES for blocks in (9, 3))


def attend(window, slots, query_raw, out_grad, own, chip, off, edges, corners, query_gain, key_gain):
    frames, width, channels = query_raw.shape
    heads = channels // LANES
    kinds = jax.ShapeDtypeStruct
    sent_shape = (chip.shape[0] + corners[0].shape[0], frames, 2, width, LANES)
    edge_shape = edges[0].shape
    most = 3 * width + span_sizes(width)[0]
    return pl.pallas_call(
        attend_kernel,
        in_specs=[whole(pltpu.SMEM)] * 2 + [whole()] * 13,
        out_specs=[whole()] * 7,
        out_shape=[
            kinds(query_raw.shape, jnp.bfloat16),
            kinds((heads, frames, 2, width, LANES), jnp.float32),
            kinds(sent_shape, jnp.bfloat16),
            kinds(sent_shape, jnp.bfloat16),
            kinds(edge_shape, jnp.float32),
            kinds(edge_shape, jnp.float32),
            kinds((2, LANES), jnp.float32),
        ],
        scratch_shapes=[
            pltpu.VMEM((GROUP, most, LANES), jnp.bfloat16),
            pltpu.VMEM((GROUP, most, LANES), jnp.bfloat16),
            pltpu.VMEM((GROUP, most, LANES), jnp.float32),
            pltpu.VMEM((GROUP, most, LANES), jnp.float32),
            pltpu.VMEM((width, span_sizes(width)[0]), jnp.float32),
        ],
        compiler_params=params(),
        name="attend",
    )(window, slots, query_raw, out_grad, own, chip, off, *edges, *corners, query_gain, key_gain)


def relay_kernel(row_slots, window_ref, slots_ref, prev_ref, next_ref, chip_ref, off_ref, prev_out, next_out):

    def one_head(g, carry):
        row_on, frame_on = window_ref[g, 1], window_ref[g, 0]
        corner_slot, frame_slot = row_slots + slots_ref[2, g], slots_ref[1, g]

        @pl.when(jnp.logical_and(frame_on == 1, row_on == 0))
        def _():
            for kept, out in ((prev_ref, prev_out), (next_ref, next_out)):
                out[frame_slot] = kept[frame_slot].astype(out.dtype)

        @pl.when(jnp.logical_and(frame_on == 1, row_on == 1))
        def _():
            for kept, out, e in ((prev_ref, prev_out, 0), (next_ref, next_out, 1)):
                terms = kept[frame_slot] + chip_ref[corner_slot, e].astype(jnp.float32)
                out[frame_slot] = (terms + off_ref[corner_slot, e].astype(jnp.float32)).astype(out.dtype)

        return carry

    lax.fori_loop(0, window_ref.shape[0], one_head, 0)


def relay(window, slots, kept, chip, off, row_slots):
    return pl.pallas_call(
        functools.partial(relay_kernel, row_slots),
        in_specs=[whole(pltpu.SMEM)] * 2 + [whole()] * 4,
        out_specs=[whole()] * 2,
        out_shape=[jax.ShapeDtypeStruct(kept[0].shape, jnp.bfloat16)] * 2,
        compiler_params=params(),
        name="add_corner_terms",
    )(window, slots, *kept, chip, off)


def finish_kernel(
    window_ref, slots_ref, key_ref, own_ref, chip_ref, off_ref, first_ref, last_ref, gain_ref,
    key_grad_ref, value_grad_ref,
):
    frames = key_ref.shape[0]
    gain_row = gain_ref[...]
    edges = (first_ref, last_ref)

    def one_head(g, carry):
        lanes = head_lanes(g)
        row_on, frame_on = window_ref[g, 1] == 1, window_ref[g, 0] == 1
        row_slot, frame_slot = slots_ref[0, g], slots_ref[1, g]
        for f in range(frames):
            sums = []
            for c in range(2):
                rows = chip_ref[row_slot, f, c].astype(jnp.float32) + off_ref[row_slot, f, c].astype(jnp.float32)
                edge = edges[f][frame_slot, c].astype(jnp.float32)
                sums.append(own_ref[g, f, c] + jnp.where(row_on, rows, 0.0) + jnp.where(frame_on, edge, 0.0))
            full_rows = key_ref[f, :, lanes].astype(jnp.float32)
            inverse = rms_inverse(full_rows)
            result = norm_backward(sums[0], full_rows * inverse, inverse, gain_row)
            key_grad_ref[f, :, lanes] = result.astype(key_grad_ref.dtype)
            value_grad_ref[f, :, lanes] = sums[1].astype(value_grad_ref.dtype)
        return carry

    lax.fori_loop(0, window_ref.shape[0], one_head, 0, unroll=4)


def finish(window, slots, key_raw, own, chip, off, edges, key_gain):
    frames, width, _ = key_raw.shape
    return pl.pallas_call(
        finish_kernel,
        in_specs=[whole(pltpu.SMEM)] * 2 + [whole()] * 7,
        out_specs=[whole()] * 2,
        out_shape=[jax.ShapeDtypeStruct(key_raw.shape, jnp.bfloat16)] * 2,
        compiler_params=params(),
        name="finish_keys",
    )(window, slots, key_raw, own, chip, off, *edges, key_gain)


def off_chip(h):
    return h + 1 if h % 2 else h - 1


def move(block, frame_step, row_rule):
    frames_size, rows_size = lax.axis_size("tm"), lax.axis_size("height")
    route = []
    for t in range(frames_size):
        for h in range(rows_size):
            to_t, to_h = t + frame_step, row_rule(h)
            if 0 <= to_t < frames_size and 0 <= to_h < rows_size:
                route.append((t * rows_size + h, to_t * rows_size + to_h))
    return lax.ppermute(block, BOTH, route)


def same_row(h):
    return h


def chip_row(h):
    return h ^ 1


def sum_over_rows(part):
    rows_size = lax.axis_size("height")
    per_row = LANES // rows_size
    pieces = part.reshape(2, rows_size, per_row).transpose(1, 0, 2).reshape(rows_size, 2 * per_row)
    return lax.all_to_all(pieces, "height", 0, 0, tiled=True).sum(0, keepdims=True)


def sum_over_frames(mine):
    copies = jnp.broadcast_to(mine, (lax.axis_size("tm"), mine.shape[1]))
    return lax.all_to_all(copies, "tm", 0, 0, tiled=True).sum(0).reshape(2, mine.shape[1] // 2)


def with_sizes(sizes, query_flat, key_flat, value_flat, grad_flat, q_gain, k_gain, window):
    slots, own, rows, first, last, corner_first, corner_last = pack(window, key_flat, value_flat, k_gain, sizes)
    off = move(rows, 0, off_chip)
    prev = move(last, 1, same_row)
    following = move(first, -1, same_row)
    off_prev = move(corner_last, 1, off_chip)
    off_next = move(corner_first, -1, off_chip)
    rows, off_prev, off_next = lax.optimization_barrier((rows, off_prev, off_next))
    chip = move(rows, 0, chip_row)
    chip_prev = move(prev, 0, chip_row)
    chip_next = move(following, 0, chip_row)

    query_grad, own_sum, chip_sum, off_sum, prev_sum, next_sum, gain_part = attend(
        window, slots, query_flat, grad_flat, own, chip, off,
        (prev, following, chip_prev, chip_next), (off_prev, off_next), q_gain, k_gain,
    )

    off_back = move(off_sum, 0, off_chip)
    chip_back = move(chip_sum, 0, chip_row)
    mine = sum_over_rows(gain_part)
    chip_back, off_back, mine = lax.optimization_barrier((chip_back, off_back, mine))
    prev_all, next_all = relay(window, slots, (prev_sum, next_sum), chip_back, off_back, sizes[0])
    last_back = move(prev_all, -1, same_row)
    first_back = move(next_all, 1, same_row)
    gain_grad = sum_over_frames(mine)
    first_back, last_back, gain_grad = lax.optimization_barrier((first_back, last_back, gain_grad))
    key_grad, value_grad = finish(
        window, slots, key_flat, own_sum, chip_back, off_back, (first_back, last_back), k_gain
    )
    return query_grad, key_grad, value_grad, gain_grad


def on_device(query_raw, key_raw, values, out_grad, query_gain, key_gain, window):
    frames, _, width, channels = query_raw.shape
    heads = channels // LANES
    flat = (frames, width, channels)
    row_on, frame_on = window[:, 1], window[:, 0]
    row_count, frame_count, both_count = jnp.sum(row_on), jnp.sum(frame_on), jnp.sum(row_on * frame_on)
    choices = SIZES + [(heads, heads, heads)]
    choice = jnp.int32(0)
    for sizes in SIZES:
        fits = (row_count <= sizes[0]) & (frame_count <= sizes[1]) & (both_count <= sizes[2])
        choice += 1 - fits.astype(jnp.int32)
    args = [x.reshape(flat) for x in (query_raw, key_raw, values, out_grad)]
    outs = lax.switch(
        choice,
        [functools.partial(with_sizes, sizes) for sizes in choices],
        *args, query_gain[None], key_gain[None], window,
    )
    return tuple(x.reshape(query_raw.shape) for x in outs[:3]) + (outs[3],)


def solution(mesh):
    token = P("tm", "height", None, None)
    return jax.shard_map(
        on_device,
        mesh=mesh,
        in_specs=(token, token, token, token, P(), P(), P()),
        out_specs=(token, token, token, P(None, "height")),
        check_vma=False,
    )
```
